512 devices in a mesh: tm: 128 (over y, z, core), grp: 4 (over x).
Axes of the slice: x: 4, y: 8, z: 8, core: 2. Of those that a mesh axis runs over, the one named last changes fastest.
Arguments:
- recording: bfloat16 [384, 524288], P(None, ('tm', 'grp')), may hold values from -6 to 6
- spatial_maps: bfloat16 [64, 384], replicated, may hold values from -0.3125 to 0.3125
- temporal_atoms: float32 [64, 64], replicated, may hold values from -0.75 to 0.75
- codes_init: float32 [64, 524288], P(None, ('tm', 'grp')), may hold values from 0 to 1
- step_sizes: float32 [64], replicated, may hold values from 0.02 to 0.08
- thresholds: float32 [64], replicated, may hold values from 0.02 to 0.3
- active_ids: int32 [512, 16], P(('tm', 'grp')), may hold values from 0 to 63, as said below
- active_counts: int32 [512], P(('tm', 'grp')), may hold values from 1 to 16, as said below
- owner_slots: int32 [64], replicated, may hold values from 0 to 255, as said below
Outputs:
- new_codes: float32 [64, 524288], P(None, ('tm', 'grp'))
- owned_panels: float32 [1024, 24576], P(('tm', 'grp'))
The draws below stay inside these ranges and needn't reach their ends.
Inputs may be any that keep to these rules, and one draw needn't show every extreme that they name: `active_ids`: the 16 atoms of one shard's list are distinct. `active_counts`: some shard's list is full. `owner_slots`: atoms of one block of 16 atoms (k // 16 equal) have distinct slots.
All inputs are finite; a program needn't handle non-finite values.
Results may differ from the reference program's by a relative error of at most 0.0034.
Values may be sent and summed in bfloat16 or wider, within the bound.
A program may use at most 64 MiB of HBM per device.

```python
import math
import jax
import jax.numpy as jnp
from jax import lax

CHANNELS = 384
TAPS = 64
ATOMS = 64
T_DEV = 1024
ACT = 16
ITERS = 3
OWN = 2
TIME = 524288
N_TM = 128
N_GRP = 4


def draw_active_ids(key, part):
    shard_total = N_TM * N_GRP
    favour = jax.random.randint(jax.random.fold_in(key, 11), (ATOMS,), 0, 4) * 65536
    noise = jax.random.randint(jax.random.fold_in(key, 12), (shard_total, ATOMS), 0, 262144)
    scores = (noise + favour[None, :]) * ATOMS + jnp.arange(ATOMS, dtype=jnp.int32)[None, :]
    best, chosen = lax.top_k(scores, ACT)
    return chosen.astype(jnp.int32)


def draw_active_counts(key, part):
    shard_total = N_TM * N_GRP
    counts = jax.random.randint(jax.random.fold_in(key, 21), (shard_total,), 1, ACT + 1)
    position = jax.random.randint(jax.random.fold_in(key, 22), (), 0, shard_total)
    counts = jnp.where(jnp.arange(shard_total, dtype=jnp.int32) == position, ACT, counts)
    return counts.astype(jnp.int32)


def draw_owner_slots(key, part):
    slot_total = N_TM * OWN
    block_size = ATOMS // N_GRP
    pieces = []
    for block_index in range(N_GRP):
        block_key = jax.random.fold_in(key, 100 + block_index)
        order = jax.random.permutation(block_key, slot_total)[:block_size].astype(jnp.int32)
        pivot = jax.random.randint(jax.random.fold_in(block_key, 1), (), 0, block_size)
        target = slot_total - 1 if block_index % 2 == 0 else 0
        order = (order - order[pivot] + target + slot_total) % slot_total
        pieces.append(order)
    return jnp.concatenate(pieces).astype(jnp.int32)


def level_of(stream_key, shape, cuts, low, top_value):
    def one(dim, parts):
        draws = jax.random.uniform(jax.random.fold_in(jax.random.fold_in(stream_key, 6), dim), (parts,), jnp.float32, low / len(cuts), top_value / len(cuts))
        return jnp.repeat(jnp.exp(draws), shape[dim] // parts).reshape((-1,) + (1,) * (len(shape) - dim - 1))

    loudness = one(*cuts[0])
    for cut in cuts[1:]:
        loudness = loudness * one(*cut)
    return loudness


def normal_values(own_key, shape, width, most, cuts=(), held_as=jnp.bfloat16):
    values = jax.random.normal(own_key, shape, jnp.float32) * width
    if len(cuts) > 0:
        values = level_of(own_key, shape, cuts, -0.22, 0.18) * values
    return jnp.clip(values, min=-most, max=most).astype(held_as)


def setup_inputs(seed: int = 0) -> dict:
    key_of = jax.random.split(jax.random.key(seed), 10)
    return {
        "recording": normal_values(key_of[0], (CHANNELS, TIME), 1.0, 6.0, ((1, 512),)),
        "spatial_maps": normal_values(key_of[1], (ATOMS, CHANNELS), CHANNELS ** -0.5, 0.3125),
        "temporal_atoms": normal_values(key_of[2], (ATOMS, TAPS), TAPS ** -0.5, 0.75, (), jnp.float32),
        "codes_init": jnp.clip(1.0 * jax.random.uniform(key_of[3], (ATOMS, TIME), jnp.float32) ** level_of(key_of[3], (ATOMS, TIME), ((1, 512),), -0.2, 0.2), 0.0, 1.0),
        "step_sizes": jnp.clip(jnp.exp(jax.random.uniform(key_of[4], (ATOMS,), jnp.float32, math.log(0.02), math.log(0.08))), 0.02, 0.08),
        "thresholds": jnp.clip(jnp.exp(jax.random.uniform(key_of[5], (ATOMS,), jnp.float32, math.log(0.02), math.log(0.3))), 0.02, 0.3),
        "active_ids": draw_active_ids(jax.random.fold_in(key_of[9], 71), 0),
        "active_counts": draw_active_counts(jax.random.fold_in(key_of[9], 71), 0),
        "owner_slots": draw_owner_slots(jax.random.fold_in(key_of[9], 71), 0),
    }


PRECISE = lax.Precision.HIGHEST


def depthwise(signal, kernel):
    return lax.conv_general_dilated(signal[None], kernel[:, None, :], (1,), "VALID", feature_group_count=kernel.shape[0], precision=PRECISE)[0]


def lagged(picked, tap_count):
    shard_len = picked.shape[1]
    padded = jnp.pad(picked, ((0, 0), (tap_count - 1, tap_count - 1)))
    return jnp.stack([padded[:, tap_count - 1 - lag: tap_count - 1 - lag + shard_len + tap_count - 1] for lag in range(tap_count)], axis=1)


def reference(recording, spatial_maps, temporal_atoms, codes_init, step_sizes, thresholds, active_ids, active_counts, owner_slots):
    tap_count = temporal_atoms.shape[1]
    atom_count = temporal_atoms.shape[0]
    projected = jnp.dot(spatial_maps, recording, preferred_element_type=jnp.float32)
    spatial_full = spatial_maps.astype(jnp.float32)
    gram_matrix = jnp.dot(spatial_full, spatial_full.T, precision=PRECISE)
    code_map = codes_init
    for sweep in range(ITERS):
        padded = jnp.pad(code_map, ((0, 0), (tap_count - 1, 0)))
        synthesis = depthwise(padded, temporal_atoms[:, ::-1])
        residual = projected - jnp.dot(gram_matrix, synthesis, precision=PRECISE)
        res_padded = jnp.pad(residual, ((0, 0), (0, tap_count - 1)))
        gradient = depthwise(res_padded, temporal_atoms)
        code_map = jnp.maximum(code_map + step_sizes[:, None] * gradient - thresholds[:, None], 0.0)
    extended = jnp.pad(recording, ((0, 0), (0, tap_count - 1)))
    scale_factor = float(T_DEV) ** -0.5
    flat_len = recording.shape[0] * tap_count

    def add_shard(totals, shard_index):
        first_col = shard_index * T_DEV
        window = lax.dynamic_slice_in_dim(extended, first_col, T_DEV + tap_count - 1, 1)
        local_codes = lax.dynamic_slice_in_dim(code_map, first_col, T_DEV, 1)
        atom_ids = lax.dynamic_index_in_dim(active_ids, shard_index, 0, keepdims=False)
        live_count = lax.dynamic_index_in_dim(active_counts, shard_index, 0, keepdims=False)
        picked = jnp.take(local_codes, atom_ids, axis=0)
        live_rows = jnp.arange(ACT, dtype=jnp.int32) < live_count
        picked = jnp.where(live_rows[:, None], picked, 0.0).astype(jnp.bfloat16)
        toeplitz = lagged(picked, tap_count)
        panel_rows = jnp.einsum("pt,alt->apl", window.astype(jnp.float32), toeplitz.astype(jnp.float32))
        panel_rows = (panel_rows * scale_factor).astype(jnp.bfloat16).reshape(ACT, flat_len)
        totals = totals.at[atom_ids].add(panel_rows.astype(jnp.float32))
        return totals, None

    totals, unused = lax.scan(add_shard, jnp.zeros((atom_count, flat_len), jnp.float32), jnp.arange(N_TM * N_GRP, dtype=jnp.int32))
    block_size = atom_count // N_GRP
    atom_index = jnp.arange(atom_count, dtype=jnp.int32)
    row_index = ((owner_slots // OWN) * N_GRP + atom_index // block_size) * OWN + owner_slots % OWN
    owned_panels = jnp.zeros((N_TM * N_GRP * OWN, flat_len), jnp.float32).at[row_index].set(totals)
    return code_map, owned_panels
```

```python
import functools

import jax
import jax.numpy as jnp
from jax import lax
from jax.experimental import pallas as pl
from jax.experimental.pallas import tpu as pltpu
from jax.sharding import PartitionSpec as P

ITERS = 3
OWN = 2
XN, YN, ZN, CN = 4, 8, 8, 2
HALO = 256
BF = jnp.bfloat16
F32 = jnp.float32
MESH = pl.DeviceIdType.MESH
VMEM = pl.BlockSpec(memory_space=pltpu.VMEM)


def dot(a, b, dims=((1,), (0,))):
    return lax.dot_general(a, b, (dims, ((), ())), preferred_element_type=F32)


def code_kernel(
    rec, maps, lags, codes0, step, thresh, select,
    codes_out, chunk,
    xb, pb, rech, send_sem, recv_sem,
):
    atoms, length = codes0.shape
    n_tm, n_grp = lax.axis_size("tm"), lax.axis_size("grp")
    shards = n_tm * n_grp
    shard = lax.axis_index("tm") * n_grp + lax.axis_index("grp")
    right, left = lax.rem(shard + 1, shards), lax.rem(shard + shards - 1, shards)
    right_id = (lax.div(right, n_grp), lax.rem(right, n_grp))
    left_id = (lax.div(left, n_grp), lax.rem(left, n_grp))

    barrier = pltpu.get_barrier_semaphore()
    for device in (left_id, right_id):
        pl.semaphore_signal(barrier, inc=1, device_id=device, device_id_type=MESH)
    pl.semaphore_wait(barrier, 2)

    def send(src, dst, index, device):
        copy = pltpu.make_async_remote_copy(
            src_ref=src,
            dst_ref=dst,
            send_sem=send_sem.at[index],
            recv_sem=recv_sem.at[index],
            device_id=device,
            device_id_type=MESH,
        )
        copy.start()
        return copy

    end = HALO + length
    width = end + HALO
    copies = [
        send(codes0.at[:, pl.ds(0, HALO)], xb.at[:, pl.ds(end, HALO)], 0, left_id),
        send(codes0.at[:, pl.ds(length - HALO, HALO)], xb.at[:, pl.ds(0, HALO)], 1, right_id),
    ]
    pb[:, HALO:end] = dot(maps[...], rec[...])
    copies += [
        send(pb.at[:, pl.ds(HALO, HALO)], pb.at[:, pl.ds(end, HALO)], 2, left_id),
        send(pb.at[:, pl.ds(end - 128, 128)], pb.at[:, pl.ds(128, 128)], 3, right_id),
        send(rec.at[:, pl.ds(0, 128)], rech, 4, left_id),
    ]
    xb[:, HALO:end] = codes0[...]

    gram = dot(maps[...], jnp.concatenate([maps[...]] * 8, axis=0), ((1,), (1,)))
    same = (
        lax.broadcasted_iota(jnp.int32, (atoms, 8 * atoms), 0)
        == lax.rem(lax.broadcasted_iota(jnp.int32, (atoms, 8 * atoms), 1), atoms)
    ).astype(F32)
    forward = jnp.concatenate([(gram * lags[i : i + 1, :]).astype(BF) for i in range(8)], axis=0)
    back = jnp.concatenate([(same * lags[i : i + 1, :]).astype(BF) for i in range(8)], axis=0)

    for copy in copies[:4]:
        copy.wait()

    first = jnp.where(shard == 0, HALO, 0)
    last = jnp.where(shard == shards - 1, end, width + HALO)

    def column(start, stop):
        return lax.broadcasted_iota(jnp.int32, (atoms, stop - start), 1) + start

    windows = [((128, width), (128, 1408)), ((128, 1408), (128, 1408)), ((HALO, 1408), (HALO, end))]
    x = jnp.where(column(0, width) < first, 0.0, xb[...])
    x_from = 0
    for (r_from, r_to), (c_from, c_to) in windows:
        x_bf = x.astype(BF)
        stacked = jnp.concatenate(
            [x_bf if j == 0 else pltpu.roll(x_bf, j, 1) for j in range(8)], axis=0
        )
        n = x.shape[1]
        z = dot(forward, stacked)
        y = z[:atoms]
        for i in range(1, 8):
            y = y + pltpu.roll(z[i * atoms : (i + 1) * atoms], 8 * i, 1)
        r = pb[:, r_from:r_to] - y[:, r_from - x_from : r_to - x_from]
        r = jnp.where(column(r_from, r_to) < last, r, 0.0)
        r_bf = r.astype(BF)
        n = r_to - r_from
        stacked = jnp.concatenate(
            [r_bf if j == 0 else pltpu.roll(r_bf, n - j, 1) for j in range(8)], axis=0
        )
        z = dot(back, stacked)
        g = z[:atoms]
        for i in range(1, 8):
            g = g + pltpu.roll(z[i * atoms : (i + 1) * atoms], n - 8 * i, 1)
        x = x[:, c_from - x_from : c_to - x_from]
        g = g[:, c_from - r_from : c_to - r_from]
        x = jnp.maximum(x + step[:, :1] * g - thresh[:, :1], 0.0)
        x = jnp.where(column(c_from, c_to) < first, 0.0, x)
        x_from = c_from
    codes_out[...] = x

    slots = select.shape[0]
    picked = dot(select[...], x.astype(BF)).astype(BF)
    picked = jnp.concatenate([picked, jnp.zeros((slots, 128), BF)], axis=1)
    shifted = jnp.concatenate(
        [picked if j == 0 else pltpu.roll(picked, j, 1) for j in range(16)], axis=0
    )
    copies[4].wait()
    after = jnp.where(shard == shards - 1, jnp.zeros_like(rech), rech[...])
    window = jnp.concatenate([rec[...], after], axis=1)
    n = length + 128
    for i in range(4):
        moved = window if i == 0 else pltpu.roll(window, n - 16 * i, 1)
        panel = dot(shifted, moved, ((1,), (1,)))
        panel = (panel * float(length) ** -0.5).astype(BF)
        for j in range(16):
            chunk[j % 8, 2 * i + j // 8] = panel[j * slots : (j + 1) * slots]


def run_codes(rec, maps, lags, codes0, step, thresh, select):
    atoms, length = codes0.shape
    channels = rec.shape[0]
    width = length + 2 * HALO
    slots = select.shape[0]
    return pl.pallas_call(
        code_kernel,
        out_shape=(
            jax.ShapeDtypeStruct((atoms, length), F32),
            jax.ShapeDtypeStruct((8, 8, slots, channels), BF),
        ),
        in_specs=[VMEM] * 7,
        out_specs=(VMEM, VMEM),
        scratch_shapes=[
            pltpu.VMEM((atoms, width), F32),
            pltpu.VMEM((atoms, width), F32),
            pltpu.VMEM((channels, 128), BF),
            pltpu.SemaphoreType.DMA((5,)),
            pltpu.SemaphoreType.DMA((5,)),
        ],
        compiler_params=pltpu.CompilerParams(
            collective_id=0, has_side_effects=True, vmem_limit_bytes=48 << 20
        ),
        name="codes",
    )(rec, maps, lags, codes0, step, thresh, select)


def sum_kernel(
    dims, chunk, tags, owners, out,
    recv1, tagr, send2, recv2, send3, recv3, tot, gath, recv5, send6, recv6,
    send_sem, recv_sem, local_sem,
):
    xn, yn, zn, cn = dims
    group = xn * cn
    atoms = send3.shape[0]
    slots = chunk.shape[2]
    block = atoms // xn
    part = atoms // zn
    tm = lax.axis_index("tm")
    x = lax.axis_index("grp")
    core = lax.rem(tm, cn)
    z = lax.rem(lax.div(tm, cn), zn)
    y = lax.div(tm, cn * zn)
    me = x * cn + core

    def device(yy, zz, cc, xx):
        return ((yy * zn + zz) * cn + cc, xx)

    pairs = []
    for o in range(1, group):
        xx, cc = lax.rem(x + o // cn, xn), lax.rem(core + o % cn, cn)
        pairs.append((xx * cn + cc, device(y, z, cc, xx)))
    ys = [lax.rem(y + o, yn) for o in range(1, yn)]
    zs = [lax.rem(z + o, zn) for o in range(1, zn)]

    barrier = pltpu.get_barrier_semaphore()
    partners = (
        [p for _, p in pairs]
        + [device(yy, z, core, x) for yy in ys]
        + [device(y, zz, core, x) for zz in zs]
    )
    for partner in partners:
        pl.semaphore_signal(barrier, inc=1, device_id=partner, device_id_type=MESH)
    pl.semaphore_wait(barrier, len(partners))

    started = []

    def send(src, dst, stage, index, target):
        copy = pltpu.make_async_remote_copy(
            src_ref=src,
            dst_ref=dst,
            send_sem=send_sem.at[stage, index],
            recv_sem=recv_sem.at[stage, index],
            device_id=target,
            device_id_type=MESH,
        )
        copy.start()
        started.append(copy)
        return copy

    first_tags = [send(tags, tagr.at[o], 0, o, p) for o, (_, p) in enumerate(pairs)]
    halves = []
    half = yn // 2
    for h in range(2):
        rows = pl.ds(h * half, half)
        own = pltpu.make_async_copy(chunk.at[me, rows], recv1.at[rows, me], local_sem.at[h])
        own.start()
        halves.append(
            [own]
            + [
                send(chunk.at[d, rows], recv1.at[rows, me], 1 + h, o, p)
                for o, (d, p) in enumerate(pairs)
            ]
        )
    for copy in first_tags:
        copy.wait_recv()
    lane = lax.broadcasted_iota(jnp.int32, (1, group * slots), 1)
    source = lax.div(lane, slots)
    row = jnp.where(source == me, tags[:1, : group * slots], -1.0)
    for o in range(1, group):
        frm = lax.rem(x - o // cn + xn, xn) * cn + lax.rem(core - o % cn + cn, cn)
        row = jnp.where(source == frm, tagr[o - 1, :1, : group * slots], row)
    atom = lax.broadcasted_iota(jnp.int32, (atoms, group * slots), 0).astype(F32)
    expand = (atom == row).astype(BF)

    for h in range(2):
        for copy in halves[h]:
            if copy is halves[h][0]:
                copy.wait()
            else:
                copy.wait_recv()
        for t in range(h * half, (h + 1) * half):
            terms = recv1[t].reshape(group * slots, recv1.shape[3])
            send2[t] = dot(expand, terms).astype(BF)
            @pl.when(y != t)
            def _():
                o = lax.rem(t - y + yn, yn) - 1
                pltpu.make_async_remote_copy(
                    src_ref=send2.at[t],
                    dst_ref=recv2.at[o],
                    send_sem=send_sem.at[3, o],
                    recv_sem=recv_sem.at[3, o],
                    device_id=device(t, z, core, x),
                    device_id_type=MESH,
                ).start()
    acc = send2[y].astype(F32)
    for o in range(yn - 1):
        copy = pltpu.make_async_remote_copy(
            src_ref=send2.at[0],
            dst_ref=recv2.at[o],
            send_sem=send_sem.at[3, o],
            recv_sem=recv_sem.at[3, o],
            device_id=device(ys[0], z, core, x),
            device_id_type=MESH,
        )
        copy.wait_recv()
        started.append(copy)
        acc = acc + recv2[o].astype(F32)
    send3[...] = acc

    third = [
        send(send3.at[pl.ds(zz * part, part)], recv3.at[o], 4, o, device(y, zz, core, x))
        for o, zz in enumerate(zs)
    ]
    mine = pl.ds(pl.multiple_of(z * part, part), part)
    acc = send3[mine]
    for o, copy in enumerate(third):
        copy.wait_recv()
        acc = acc + recv3[o]
    tot[...] = acc

    gath[mine] = acc
    fourth = [
        send(tot, gath.at[mine], 5, o, device(y, zz, core, x))
        for o, zz in enumerate(zs)
    ]
    for copy in fourth:
        copy.wait_recv()

    own = pltpu.make_async_copy(gath.at[pl.ds(x * block, block)], recv5.at[me], local_sem.at[2])
    own.start()
    fifth = [
        send(gath.at[pl.ds(lax.div(d, cn) * block, block)], recv5.at[me], 6, o, p)
        for o, (d, p) in enumerate(pairs)
    ]
    own.wait()
    for copy in fifth:
        copy.wait_recv()

    rows_n = yn * OWN * group
    cols_n = group * block
    r = lax.broadcasted_iota(jnp.int32, (rows_n, cols_n), 0)
    c = lax.broadcasted_iota(jnp.int32, (rows_n, cols_n), 1)
    wanted_y = lax.div(r, OWN * group)
    wanted_slot = lax.rem(lax.div(r, group), OWN)
    wanted = ((wanted_y * zn + z) * cn + core) * OWN + wanted_slot
    hit = (owners[:1, :cols_n] == wanted.astype(F32)) & (lax.rem(r, group) == lax.div(c, block))
    sums = recv5[...].reshape(cols_n, recv5.shape[2])
    rows = dot(hit.astype(BF), sums.astype(BF))
    send6[...] = rows.astype(BF).reshape(send6.shape)
    sixth = [
        send(send6.at[yy], recv6.at[y], 7, o, device(yy, z, core, x))
        for o, yy in enumerate(ys)
    ]
    recv6[y] = send6[y]
    for copy in sixth:
        copy.wait_recv()
    out[...] = recv6[...].astype(F32)
    for copy in started:
        copy.wait_send()


def run_sums(chunk, tags, owners, atoms, dims):
    xn, yn, zn, cn = dims
    group = xn * cn
    slots, channels = chunk.shape[2:]
    block = atoms // xn
    part = atoms // zn
    most = max(group, yn, zn) - 1
    return pl.pallas_call(
        functools.partial(sum_kernel, dims),
        out_shape=jax.ShapeDtypeStruct((yn, OWN * group, channels), F32),
        in_specs=[VMEM] * 3,
        out_specs=VMEM,
        scratch_shapes=[
            pltpu.VMEM((yn, group, slots, channels), BF),
            pltpu.VMEM((group - 1,) + tags.shape, F32),
            pltpu.VMEM((yn, atoms, channels), BF),
            pltpu.VMEM((yn - 1, atoms, channels), BF),
            pltpu.VMEM((atoms, channels), F32),
            pltpu.VMEM((zn - 1, part, channels), F32),
            pltpu.VMEM((part, channels), F32),
            pltpu.VMEM((atoms, channels), F32),
            pltpu.VMEM((group, block, channels), F32),
            pltpu.VMEM((yn, OWN * group, channels), BF),
            pltpu.VMEM((yn, OWN * group, channels), BF),
            pltpu.SemaphoreType.DMA((8, most)),
            pltpu.SemaphoreType.DMA((8, most)),
            pltpu.SemaphoreType.DMA((3,)),
        ],
        compiler_params=pltpu.CompilerParams(
            collective_id=1, has_side_effects=True, vmem_limit_bytes=48 << 20
        ),
        name="sums",
    )(chunk, tags, owners)


def body(
    recording,
    spatial_maps,
    temporal_atoms,
    codes_init,
    step_sizes,
    thresholds,
    active_ids,
    active_counts,
    owner_slots,
):
    atoms, taps = temporal_atoms.shape
    channels = recording.shape[0]
    dims = (XN, YN, ZN, CN)
    group = XN * CN
    block = atoms // XN
    slots = active_ids.shape[1]
    lags = temporal_atoms.T.reshape(8, 8 * atoms)
    live = jnp.arange(slots) < active_counts[0]
    ids = jnp.where(live, active_ids[0], -1)
    select = (ids[:, None] == jnp.arange(atoms)[None, :]).astype(BF)
    step = jnp.broadcast_to(step_sizes[:, None], (atoms, 128))
    thresh = jnp.broadcast_to(thresholds[:, None], (atoms, 128))
    tags = jnp.broadcast_to(jnp.tile(ids.astype(F32), group)[None, :], (8, group * slots))
    block_owner = lax.dynamic_slice_in_dim(owner_slots, lax.axis_index("grp") * block, block)
    owners = jnp.broadcast_to(
        jnp.tile(block_owner.astype(F32), group)[None, :], (8, group * block)
    )
    codes, chunk = run_codes(recording, spatial_maps, lags, codes_init, step, thresh, select)
    rows = run_sums(chunk, tags, owners, atoms, dims)
    panels = rows.reshape(YN, OWN, group, channels).transpose(1, 3, 0, 2)
    return codes, panels.reshape(OWN, channels * taps)


def solution(mesh):
    in_specs = (
        P(None, ("tm", "grp")),
        P(),
        P(),
        P(None, ("tm", "grp")),
        P(),
        P(),
        P(("tm", "grp"), None),
        P(("tm", "grp")),
        P(),
    )
    out_specs = (P(None, ("tm", "grp")), P(("tm", "grp"), None))
    return jax.shard_map(body, mesh=mesh, in_specs=in_specs, out_specs=out_specs, check_vma=False)
```

```python
import functools

import jax
import jax.numpy as jnp
from jax import lax
from jax.experimental import pallas as pl
from jax.experimental.pallas import tpu as pltpu
from jax.sharding import PartitionSpec as P

OWN = 2
XN, YN, ZN, CN = 4, 8, 8, 2
GROUP = XN * CN
HALO = 256
BF = jnp.bfloat16
F32 = jnp.float32
MESH = pl.DeviceIdType.MESH
HBM = pl.BlockSpec(memory_space=pl.ANY)
VMEM = pl.BlockSpec(memory_space=pltpu.VMEM)


def dot(a, b, dims=((1,), (0,))):
    return lax.dot_general(a, b, (dims, ((), ())), preferred_element_type=F32)


def split(v):
    high = v.astype(BF)
    return high, (v - high.astype(F32)).astype(BF)


def iota(shape, dim):
    return lax.broadcasted_iota(jnp.int32, shape, dim)


def to_column(row):
    n = row.shape[1]
    eye = iota((n, n), 0) == iota((n, n), 1)
    return jnp.sum(jnp.where(eye, jnp.broadcast_to(row, (n, n)), 0.0), axis=1, keepdims=True)


def kernel(
    rec_hbm, maps_hbm, waves_hbm, codes_hbm, step_hbm, thresh_hbm, ids_hbm, counts_hbm, owners_hbm,
    codes_out, panels_out,
    rec, maps, waves, step_row, thresh_row, ids_row, counts_row, owners_row,
    xb, pb, rech, tags, tagr, chunk, recv1, send2, recv2, send3, recv3, tot, recv4, send5, recv5,
    send6, recv6, turned, in_sem, send_sem, recv_sem,
):
    slots = ids_row.shape[1]
    channels, length = rec.shape
    atoms = maps.shape[0]
    block = atoms // XN
    part = atoms // ZN
    n_tm, n_grp = lax.axis_size("tm"), lax.axis_size("grp")
    shards = n_tm * n_grp
    tm = lax.axis_index("tm")
    x = lax.axis_index("grp")
    core = lax.rem(tm, CN)
    z = lax.rem(lax.div(tm, CN), ZN)
    y = lax.div(tm, CN * ZN)
    me = x * CN + core
    shard = tm * n_grp + x

    def device(yy, zz, cc, xx):
        return ((yy * ZN + zz) * CN + cc, xx)

    right, left = lax.rem(shard + 1, shards), lax.rem(shard + shards - 1, shards)
    right_id = (lax.div(right, n_grp), lax.rem(right, n_grp))
    left_id = (lax.div(left, n_grp), lax.rem(left, n_grp))
    pairs = []
    for o in range(1, GROUP):
        xx, cc = lax.rem(x + o // CN, XN), lax.rem(core + o % CN, CN)
        pairs.append((xx * CN + cc, device(y, z, cc, xx)))
    sibling = device(y, z, 1 - core, x)
    ys = [lax.rem(y + o, YN) for o in range(1, YN)]
    zs = [lax.rem(z + o, ZN) for o in range(1, ZN)]
    home = lax.div(z * part, block)
    per = block // part
    at_home = x == home

    barrier = pltpu.get_barrier_semaphore()

    def greet(target):
        pl.semaphore_signal(barrier, inc=1, device_id=target, device_id_type=MESH)

    partners = (
        [left_id, right_id]
        + [p for _, p in pairs]
        + [device(yy, z, core, x) for yy in ys]
        + [device(y, zz, core, x) for zz in zs]
    )
    for partner in partners:
        greet(partner)
    for xx in range(XN):
        for q in range(per):
            zz = x * per + q

            @pl.when(jnp.logical_not((x == xx) & (z == zz)))
            def _():
                greet(device(y, zz, core, xx))

    loads = [
        pltpu.make_async_copy(src, dst, in_sem.at[i])
        for i, (src, dst) in enumerate(
            [
                (codes_hbm, xb.at[:, pl.ds(HALO, length)]),
                (rec_hbm, rec),
                (maps_hbm, maps),
                (waves_hbm, waves),
                (step_hbm, step_row),
                (thresh_hbm, thresh_row),
                (ids_hbm, ids_row),
                (counts_hbm, counts_row),
                (owners_hbm, owners_row),
            ]
        )
    ]
    for load in loads:
        load.start()
    for load in loads:
        load.wait()

    started = []

    def copy_to(src, dst, stage, index, target, recv_index=None):
        return pltpu.make_async_remote_copy(
            src_ref=src,
            dst_ref=dst,
            send_sem=send_sem.at[stage, index],
            recv_sem=recv_sem.at[stage, index if recv_index is None else recv_index],
            device_id=target,
            device_id_type=MESH,
        )

    def send(*args):
        copy = copy_to(*args)
        copy.start()
        started.append(copy)
        return copy

    end = HALO + length
    width = end + HALO
    pb[:, HALO:end] = dot(maps[...], rec[...])
    pb[:, :128] = jnp.zeros((atoms, 128), F32)

    live = iota((1, slots), 1) < jnp.broadcast_to(counts_row[...], (1, slots))
    ids = jnp.where(live, ids_row[...].astype(F32), -1.0)
    tags[...] = jnp.broadcast_to(jnp.concatenate([ids] * GROUP, axis=1), tags.shape)
    select = (iota((slots, atoms), 1).astype(F32) == to_column(ids)).astype(BF)

    pl.semaphore_wait(barrier, len(partners) + ZN - jnp.where(at_home, 1, 0))

    halo = [
        send(xb.at[:, pl.ds(HALO, HALO)], xb.at[:, pl.ds(end, HALO)], 0, 0, left_id),
        send(xb.at[:, pl.ds(length, HALO)], xb.at[:, pl.ds(0, HALO)], 0, 1, right_id),
        send(pb.at[:, pl.ds(HALO, HALO)], pb.at[:, pl.ds(end, HALO)], 0, 2, left_id),
        send(pb.at[:, pl.ds(end - 128, 128)], pb.at[:, pl.ds(128, 128)], 0, 3, right_id),
    ]

    half = atoms // 2
    lanes = 8 * half
    pick_lag = iota((64, 8 * lanes), 1)
    pick_lag = lax.div(pick_lag, lanes) * 8 + lax.div(lax.rem(pick_lag, lanes), half)
    pick_lag = (pick_lag == iota((64, 8 * lanes), 0)).astype(BF)
    same = (iota((half, lanes), 0) == lax.rem(iota((half, lanes), 1), half)).astype(F32)
    spread = [dot(v, pick_lag) for v in split(waves[...])]
    filters = []
    for g in range(2):
        high, low = [
            jnp.concatenate(
                [
                    (v[g * half : (g + 1) * half, i * lanes : (i + 1) * lanes] * same).astype(BF)
                    for i in range(8)
                ],
                axis=0,
            )
            for v in spread
        ]
        filters.append(jnp.concatenate([high, high, low], axis=1))
    high, low = split(dot(maps[...], maps[...], ((1,), (1,))))
    gram = jnp.concatenate([high, high, low], axis=1)
    step = to_column(step_row[...])
    thresh = to_column(thresh_row[...])

    def depthwise(v, sign):
        n = v.shape[1]
        rolled = [
            [u if j == 0 else pltpu.roll(u, (sign * j) % n, 1) for j in range(8)] for u in split(v)
        ]
        groups = []
        for g in range(2):
            high, low = [
                jnp.concatenate([u[g * half : (g + 1) * half] for u in us], axis=0) for us in rolled
            ]
            w = dot(filters[g], jnp.concatenate([high, low, high], axis=0))
            total = w[:half]
            for i in range(1, 8):
                total = total + pltpu.roll(w[i * half : (i + 1) * half], (sign * 8 * i) % n, 1)
            groups.append(total)
        return jnp.concatenate(groups, axis=0)

    for copy in halo:
        copy.wait_recv()
    more = [
        send(rec.at[:, pl.ds(0, 128)], rech, 0, 4, left_id),
    ]
    tag_copies = [send(tags, tagr.at[o], 1, o, p) for o, (_, p) in enumerate(pairs)]

    first = jnp.where(shard == 0, HALO, 0)
    last = jnp.where(shard == shards - 1, end, width + HALO)

    def column(start, stop):
        return iota((atoms, stop - start), 1) + start

    windows = [((128, width), (128, 1408)), ((128, 1408), (128, 1408)), ((HALO, 1408), (HALO, end))]
    v = jnp.where(column(0, width) < first, 0.0, xb[...])
    v_from = 0
    for (r_from, r_to), (c_from, c_to) in windows:
        synthesis = depthwise(v, 1)[:, r_from - v_from : r_to - v_from]
        high, low = split(synthesis)
        r = pb[:, r_from:r_to] - dot(gram, jnp.concatenate([high, low, high], axis=0))
        r = jnp.where(column(r_from, r_to) < last, r, 0.0)
        g = depthwise(r, -1)[:, c_from - r_from : c_to - r_from]
        v = v[:, c_from - v_from : c_to - v_from]
        v = jnp.maximum(v + step * g - thresh, 0.0)
        v = jnp.where(column(c_from, c_to) < first, 0.0, v)
        v_from = c_from
    codes_out[...] = v

    picked = dot(select, v.astype(BF)).astype(BF)
    picked = jnp.concatenate([picked, jnp.zeros((slots, 128), BF)], axis=1)
    shifted = jnp.concatenate(
        [picked if j == 0 else pltpu.roll(picked, j, 1) for j in range(16)], axis=0
    )
    more[0].wait_recv()
    after = jnp.where(shard == shards - 1, jnp.zeros_like(rech), rech[...])
    window = jnp.concatenate([rec[...], after], axis=1)
    n = length + 128
    pieces = YN // 2
    order = [lax.rem(lax.div(y, 2) + p + 1, pieces) for p in range(pieces)]
    firsts = []
    for p in range(pieces):
        i = order[p]
        moved = pltpu.roll(window, lax.rem(n - 16 * i, n), 1)
        panel = dot(shifted, moved, ((1,), (1,)))
        panel = (panel * float(length) ** -0.5).astype(BF)
        for j in range(16):
            chunk[j % 8, 2 * i + j // 8] = panel[j * slots : (j + 1) * slots]
        rows = pl.ds(2 * i, 2)
        firsts.append(
            [
                send(chunk.at[d, rows], recv1.at[rows, me], 2 + p, o, target)
                for o, (d, target) in enumerate(pairs)
            ]
        )
        recv1[rows, me] = chunk[me, rows]

    for copy in tag_copies:
        copy.wait_recv()
    lane = iota((1, GROUP * slots), 1)
    source = lax.div(lane, slots)
    row = jnp.where(source == me, tags[:1], -1.0)
    for o in range(1, GROUP):
        frm = lax.rem(x - o // CN + XN, XN) * CN + lax.rem(core - o % CN + CN, CN)
        row = jnp.where(source == frm, tagr[o - 1, :1], row)
    expand = (iota((atoms, GROUP * slots), 0).astype(F32) == row).astype(BF)
    for p in range(pieces):
        for copy in firsts[p]:
            copy.wait_recv()
        for q in range(2):
            t = 2 * order[p] + q
            terms = recv1[t].reshape(GROUP * slots, channels)
            send2[t] = dot(expand, terms).astype(BF)
            o = lax.rem(t - y + YN, YN)

            @pl.when(o != 0)
            def _():
                copy_to(send2.at[t], recv2.at[o - 1], 6, o - 1, device(t, z, core, x)).start()

    acc = send2[y].astype(F32)
    for o in range(YN - 1):
        copy = copy_to(send2.at[0], recv2.at[o], 6, o, device(ys[0], z, core, x))
        copy.wait_recv()
        started.append(copy)
        acc = acc + recv2[o].astype(F32)
    send3[...] = acc

    third = [
        send(send3.at[pl.ds(zz * part, part)], recv3.at[o], 7, o, device(y, zz, core, x))
        for o, zz in enumerate(zs)
    ]
    acc = send3[pl.ds(pl.multiple_of(z * part, part), part)]
    for o, copy in enumerate(third):
        copy.wait_recv()
        acc = acc + recv3[o]
    tot[...] = acc

    place = x * per + lax.rem(z, per)
    fourth = []
    for o in range(ZN):
        zz = lax.rem(z + o, ZN)
        copy = copy_to(tot, recv4.at[place], 8, o, device(y, zz, core, home), place)
        fourth.append(copy)
        if o == 0:

            @pl.when(jnp.logical_not(at_home))
            def _():
                copy.start()

            @pl.when(at_home)
            def _():
                recv4[place] = tot[...]
        else:
            copy.start()
    for xx in range(XN):
        for q in range(per):
            k = xx * per + q
            copy = copy_to(tot, recv4.at[k], 8, 0, sibling, k)

            @pl.when(jnp.logical_not((x == xx) & (z == x * per + q)))
            def _():
                copy.wait_recv()

    send5[...] = recv4[...].reshape(XN * block, channels).astype(BF)
    fifth = send(send5, recv5, 9, 0, sibling)
    rows_n = YN * OWN * GROUP
    cols_n = GROUP * block
    half_n = XN * block
    block_owner = owners_row[:, :block]
    for b in range(1, XN):
        block_owner = jnp.where(x == b, owners_row[:, b * block : (b + 1) * block], block_owner)
    block_owner = jnp.concatenate([block_owner.astype(F32)] * GROUP, axis=1)
    r = iota((rows_n, cols_n), 0)
    c = iota((rows_n, cols_n), 1)
    wanted_slot = lax.rem(lax.div(r, GROUP), OWN)
    wanted = ((lax.div(r, OWN * GROUP) * ZN + z) * CN + core) * OWN + wanted_slot
    c_core = jnp.where(c < half_n, core, 1 - core)
    c_group = lax.div(lax.rem(c, half_n), block) * CN + c_core
    hit = (block_owner == wanted.astype(F32)) & (lax.rem(r, GROUP) == c_group)
    hit = hit.astype(BF)
    fifth.wait_recv()

    sums = jnp.concatenate([send5[...], recv5[...]], axis=0)
    send6[...] = dot(hit, sums).astype(BF).reshape(send6.shape)
    sixth = [
        send(send6.at[yy], recv6.at[y], 10, o, device(yy, z, core, x)) for o, yy in enumerate(ys)
    ]
    recv6[y] = send6[y]
    for copy in sixth:
        copy.wait_recv()

    held = recv6[...].astype(F32)
    taps = YN * GROUP
    table = jnp.concatenate(
        [held[:, s * GROUP : (s + 1) * GROUP].reshape(taps, channels) for s in range(OWN)], axis=0
    )
    turned[...] = table.T
    even = turned[pl.ds(0, channels // 2, stride=2), :]
    odd = turned[pl.ds(1, channels // 2, stride=2), :]
    low_lanes = iota(even.shape, 1) < taps
    slot0 = jnp.where(low_lanes, even, pltpu.roll(odd, taps, 1))
    slot1 = jnp.where(low_lanes, pltpu.roll(even, taps, 1), odd)
    for q in range(channels // 2):
        panels_out[:, q * 128 : (q + 1) * 128] = jnp.concatenate(
            [slot0[q : q + 1], slot1[q : q + 1]], axis=0
        )

    for copy in started:
        copy.wait_send()
    for o, copy in enumerate(fourth):
        if o == 0:

            @pl.when(jnp.logical_not(at_home))
            def _():
                copy.wait_send()
        else:
            copy.wait_send()


def body(
    recording,
    spatial_maps,
    temporal_atoms,
    codes_init,
    step_sizes,
    thresholds,
    active_ids,
    active_counts,
    owner_slots,
):
    atoms, taps = temporal_atoms.shape
    channels, length = recording.shape
    slots = active_ids.shape[1]
    width = length + 2 * HALO
    block, part = atoms // XN, atoms // ZN
    return pl.pallas_call(
        kernel,
        out_shape=(
            jax.ShapeDtypeStruct((atoms, length), F32),
            jax.ShapeDtypeStruct((OWN, channels * taps), F32),
        ),
        in_specs=[HBM] * 9,
        out_specs=(VMEM, VMEM),
        scratch_shapes=[
            pltpu.VMEM((channels, length), BF),
            pltpu.VMEM((atoms, channels), BF),
            pltpu.VMEM((atoms, taps), F32),
            pltpu.VMEM((1, atoms), F32),
            pltpu.VMEM((1, atoms), F32),
            pltpu.VMEM((1, slots), jnp.int32),
            pltpu.VMEM((1, 1), jnp.int32),
            pltpu.VMEM((1, atoms), jnp.int32),
            pltpu.VMEM((atoms, width), F32),
            pltpu.VMEM((atoms, width), F32),
            pltpu.VMEM((channels, 128), BF),
            pltpu.VMEM((8, GROUP * slots), F32),
            pltpu.VMEM((GROUP - 1, 8, GROUP * slots), F32),
            pltpu.VMEM((GROUP, YN, slots, channels), BF),
            pltpu.VMEM((YN, GROUP, slots, channels), BF),
            pltpu.VMEM((YN, atoms, channels), BF),
            pltpu.VMEM((YN - 1, atoms, channels), BF),
            pltpu.VMEM((atoms, channels), F32),
            pltpu.VMEM((ZN - 1, part, channels), F32),
            pltpu.VMEM((part, channels), F32),
            pltpu.VMEM((XN * block // part, part, channels), F32),
            pltpu.VMEM((XN * block, channels), BF),
            pltpu.VMEM((XN * block, channels), BF),
            pltpu.VMEM((YN, OWN * GROUP, channels), BF),
            pltpu.VMEM((YN, OWN * GROUP, channels), BF),
            pltpu.VMEM((channels, OWN * taps), F32),
            pltpu.SemaphoreType.DMA((9,)),
            pltpu.SemaphoreType.DMA((11, 8)),
            pltpu.SemaphoreType.DMA((11, 8)),
        ],
        compiler_params=pltpu.CompilerParams(
            collective_id=0, has_side_effects=True, vmem_limit_bytes=56 << 20
        ),
        name="codes_and_panels",
    )(
        recording,
        spatial_maps,
        temporal_atoms,
        codes_init,
        step_sizes.reshape(1, atoms),
        thresholds.reshape(1, atoms),
        active_ids,
        active_counts.reshape(1, 1),
        owner_slots.reshape(1, atoms),
    )


def solution(mesh):
    in_specs = (
        P(None, ("tm", "grp")),
        P(),
        P(),
        P(None, ("tm", "grp")),
        P(),
        P(),
        P(("tm", "grp"), None),
        P(("tm", "grp")),
        P(),
    )
    out_specs = (P(None, ("tm", "grp")), P(("tm", "grp"), None))
    return jax.shard_map(body, mesh=mesh, in_specs=in_specs, out_specs=out_specs, check_vma=False)
```

```python
import functools

import jax
import jax.numpy as jnp
from jax import lax
from jax.experimental import pallas as pl
from jax.experimental.pallas import tpu as pltpu
from jax.sharding import PartitionSpec as P

OWN = 2
XN, YN, ZN, CN = 4, 8, 8, 2
GROUP = XN * CN
HALO = 256
BF = jnp.bfloat16
F32 = jnp.float32
MESH = pl.DeviceIdType.MESH
HBM = pl.BlockSpec(memory_space=pl.ANY)
VMEM = pl.BlockSpec(memory_space=pltpu.VMEM)


def dot(a, b, dims=((1,), (0,))):
    return lax.dot_general(a, b, (dims, ((), ())), preferred_element_type=F32)


def split(v):
    high = v.astype(BF)
    return high, (v - high.astype(F32)).astype(BF)


def iota(shape, dim):
    return lax.broadcasted_iota(jnp.int32, shape, dim)


def to_column(row):
    n = row.shape[1]
    eye = iota((n, n), 0) == iota((n, n), 1)
    return jnp.sum(jnp.where(eye, jnp.broadcast_to(row, (n, n)), 0.0), axis=1, keepdims=True)


def kernel(
    rec_hbm, maps_hbm, waves_hbm, codes_hbm, step_hbm, thresh_hbm, ids_hbm, counts_hbm, owners_hbm,
    codes_out, panels_out,
    rec, maps, waves, step_row, thresh_row, ids_row, counts_row, owners_row,
    xb, pb, rech, tags, tagr, chunk, recv1, send2, recv2, send3, recv3, tot, recv4, send5, recv5,
    send6, recv6, turned, in_sem, send_sem, recv_sem,
):
    slots = ids_row.shape[1]
    channels, length = rec.shape
    atoms = maps.shape[0]
    block = atoms // XN
    part = atoms // ZN
    n_tm, n_grp = lax.axis_size("tm"), lax.axis_size("grp")
    shards = n_tm * n_grp
    tm = lax.axis_index("tm")
    x = lax.axis_index("grp")
    core = lax.rem(tm, CN)
    z = lax.rem(lax.div(tm, CN), ZN)
    y = lax.div(tm, CN * ZN)
    me = x * CN + core
    shard = tm * n_grp + x

    def device(yy, zz, cc, xx):
        return ((yy * ZN + zz) * CN + cc, xx)

    right, left = lax.rem(shard + 1, shards), lax.rem(shard + shards - 1, shards)
    right_id = (lax.div(right, n_grp), lax.rem(right, n_grp))
    left_id = (lax.div(left, n_grp), lax.rem(left, n_grp))
    pairs = []
    for o in range(1, GROUP):
        xx, cc = lax.rem(x + o // CN, XN), lax.rem(core + o % CN, CN)
        pairs.append((xx * CN + cc, device(y, z, cc, xx)))
    sibling = device(y, z, 1 - core, x)
    ys = [lax.rem(y + o, YN) for o in range(1, YN)]
    zs = [lax.rem(z + o, ZN) for o in range(1, ZN)]
    home = lax.div(z * part, block)
    per = block // part
    at_home = x == home

    barrier = pltpu.get_barrier_semaphore()

    def greet(target):
        pl.semaphore_signal(barrier, inc=1, device_id=target, device_id_type=MESH)

    partners = (
        [left_id, right_id]
        + [p for _, p in pairs]
        + [device(yy, z, core, x) for yy in ys]
        + [device(y, zz, core, x) for zz in zs]
    )
    for partner in partners:
        greet(partner)
    for xx in range(XN):
        for q in range(per):
            zz = x * per + q

            @pl.when(jnp.logical_not((x == xx) & (z == zz)))
            def _():
                greet(device(y, zz, core, xx))

    loads = [
        pltpu.make_async_copy(src, dst, in_sem.at[i])
        for i, (src, dst) in enumerate(
            [
                (codes_hbm, xb.at[:, pl.ds(HALO, length)]),
                (rec_hbm, rec),
                (maps_hbm, maps),
                (waves_hbm, waves),
                (step_hbm, step_row),
                (thresh_hbm, thresh_row),
                (ids_hbm, ids_row),
                (counts_hbm, counts_row),
                (owners_hbm, owners_row),
            ]
        )
    ]
    for load in loads:
        load.start()

    started = []

    def copy_to(src, dst, stage, index, target, recv_index=None):
        return pltpu.make_async_remote_copy(
            src_ref=src,
            dst_ref=dst,
            send_sem=send_sem.at[stage, index],
            recv_sem=recv_sem.at[stage, index if recv_index is None else recv_index],
            device_id=target,
            device_id_type=MESH,
        )

    def send(*args):
        copy = copy_to(*args)
        copy.start()
        started.append(copy)
        return copy

    end = HALO + length
    width = end + HALO
    pl.semaphore_wait(barrier, len(partners) + ZN - jnp.where(at_home, 1, 0))
    halo = [
        send(codes_hbm.at[:, pl.ds(0, HALO)], xb.at[:, pl.ds(end, HALO)], 0, 0, left_id),
        send(codes_hbm.at[:, pl.ds(length - HALO, HALO)], xb.at[:, pl.ds(0, HALO)], 0, 1, right_id),
    ]
    for load in loads:
        load.wait()
    pb[:, HALO:end] = dot(maps[...], rec[...])
    halo += [
        send(pb.at[:, pl.ds(HALO, HALO)], pb.at[:, pl.ds(end, HALO)], 0, 2, left_id),
        send(pb.at[:, pl.ds(end - 128, 128)], pb.at[:, pl.ds(128, 128)], 0, 3, right_id),
    ]
    pb[:, :128] = jnp.zeros((atoms, 128), F32)

    live = iota((1, slots), 1) < jnp.broadcast_to(counts_row[...], (1, slots))
    ids = jnp.where(live, ids_row[...].astype(F32), -1.0)
    tags[...] = jnp.broadcast_to(jnp.concatenate([ids] * GROUP, axis=1), tags.shape)
    select = (iota((slots, atoms), 1).astype(F32) == to_column(ids)).astype(BF)

    half = atoms // 2
    lanes = 8 * half
    pick_lag = iota((64, 8 * lanes), 1)
    pick_lag = lax.div(pick_lag, lanes) * 8 + lax.div(lax.rem(pick_lag, lanes), half)
    pick_lag = (pick_lag == iota((64, 8 * lanes), 0)).astype(BF)
    same = (iota((half, lanes), 0) == lax.rem(iota((half, lanes), 1), half)).astype(F32)
    spread = [dot(v, pick_lag) for v in split(waves[...])]
    filters = []
    for g in range(2):
        high, low = [
            jnp.concatenate(
                [
                    (v[g * half : (g + 1) * half, i * lanes : (i + 1) * lanes] * same).astype(BF)
                    for i in range(8)
                ],
                axis=0,
            )
            for v in spread
        ]
        filters.append(jnp.concatenate([high, high, low], axis=1))
    high, low = split(dot(maps[...], maps[...], ((1,), (1,))))
    gram = jnp.concatenate([high, high, low], axis=1)
    step = to_column(step_row[...])
    thresh = to_column(thresh_row[...])

    def depthwise(v, sign):
        n = v.shape[1]
        rolled = [
            [u if j == 0 else pltpu.roll(u, (sign * j) % n, 1) for j in range(8)] for u in split(v)
        ]
        groups = []
        for g in range(2):
            high, low = [
                jnp.concatenate([u[g * half : (g + 1) * half] for u in us], axis=0) for us in rolled
            ]
            w = dot(filters[g], jnp.concatenate([high, low, high], axis=0))
            total = w[:half]
            for i in range(1, 8):
                total = total + pltpu.roll(w[i * half : (i + 1) * half], (sign * 8 * i) % n, 1)
            groups.append(total)
        return jnp.concatenate(groups, axis=0)

    for copy in halo:
        copy.wait_recv()
    more = [
        send(rec.at[:, pl.ds(0, 128)], rech, 0, 4, left_id),
    ]
    tag_copies = [send(tags, tagr.at[o], 1, o, p) for o, (_, p) in enumerate(pairs)]

    first = jnp.where(shard == 0, HALO, 0)
    last = jnp.where(shard == shards - 1, end, width + HALO)

    def column(start, stop):
        return iota((atoms, stop - start), 1) + start

    windows = [((128, width), (128, 1408)), ((128, 1408), (128, 1408)), ((HALO, 1408), (HALO, end))]
    v = jnp.where(column(0, width) < first, 0.0, xb[...])
    v_from = 0
    for (r_from, r_to), (c_from, c_to) in windows:
        synthesis = depthwise(v, 1)[:, r_from - v_from : r_to - v_from]
        high, low = split(synthesis)
        r = pb[:, r_from:r_to] - dot(gram, jnp.concatenate([high, low, high], axis=0))
        r = jnp.where(column(r_from, r_to) < last, r, 0.0)
        g = depthwise(r, -1)[:, c_from - r_from : c_to - r_from]
        v = v[:, c_from - v_from : c_to - v_from]
        v = jnp.maximum(v + step * g - thresh, 0.0)
        v = jnp.where(column(c_from, c_to) < first, 0.0, v)
        v_from = c_from
    codes_out[...] = v

    picked = dot(select, v.astype(BF)).astype(BF)
    picked = jnp.concatenate([picked, jnp.zeros((slots, 128), BF)], axis=1)
    shifted = jnp.concatenate(
        [picked if j == 0 else pltpu.roll(picked, j, 1) for j in range(16)], axis=0
    )
    more[0].wait_recv()
    after = jnp.where(shard == shards - 1, jnp.zeros_like(rech), rech[...])
    window = jnp.concatenate([rec[...], after], axis=1)
    n = length + 128
    pieces = YN // 2
    order = [lax.rem(lax.div(y, 2) + p + 1, pieces) for p in range(pieces)]
    firsts = []
    for p in range(pieces):
        i = order[p]
        moved = pltpu.roll(window, lax.rem(n - 16 * i, n), 1)
        panel = dot(shifted, moved, ((1,), (1,)))
        panel = (panel * float(length) ** -0.5).astype(BF)
        for j in range(16):
            chunk[j % 8, 2 * i + j // 8] = panel[j * slots : (j + 1) * slots]
        rows = pl.ds(2 * i, 2)
        firsts.append(
            [
                send(chunk.at[d, rows], recv1.at[rows, me], 2 + p, o, target)
                for o, (d, target) in enumerate(pairs)
            ]
        )
        recv1[rows, me] = chunk[me, rows]

    for copy in tag_copies:
        copy.wait_recv()
    lane = iota((1, GROUP * slots), 1)
    source = lax.div(lane, slots)
    row = jnp.where(source == me, tags[:1], -1.0)
    for o in range(1, GROUP):
        frm = lax.rem(x - o // CN + XN, XN) * CN + lax.rem(core - o % CN + CN, CN)
        row = jnp.where(source == frm, tagr[o - 1, :1], row)
    expand = (iota((atoms, GROUP * slots), 0).astype(F32) == row).astype(BF)
    for p in range(pieces):
        for copy in firsts[p]:
            copy.wait_recv()
        for q in range(2):
            t = 2 * order[p] + q
            terms = recv1[t].reshape(GROUP * slots, channels)
            send2[t] = dot(expand, terms).astype(BF)
            o = lax.rem(t - y + YN, YN)

            @pl.when(o != 0)
            def _():
                copy_to(send2.at[t], recv2.at[o - 1], 6, o - 1, device(t, z, core, x)).start()

    acc = send2[y].astype(F32)
    for o in range(YN - 1):
        copy = copy_to(send2.at[0], recv2.at[o], 6, o, device(ys[0], z, core, x))
        copy.wait_recv()
        started.append(copy)
        acc = acc + recv2[o].astype(F32)
    send3[...] = acc

    third = [
        send(send3.at[pl.ds(zz * part, part)], recv3.at[o], 7, o, device(y, zz, core, x))
        for o, zz in enumerate(zs)
    ]
    acc = send3[pl.ds(pl.multiple_of(z * part, part), part)]
    for o, copy in enumerate(third):
        copy.wait_recv()
        acc = acc + recv3[o]
    tot[...] = acc

    place = x * per + lax.rem(z, per)
    fourth = []
    for o in range(ZN):
        zz = lax.rem(z + o, ZN)
        copy = copy_to(tot, recv4.at[place], 8, o, device(y, zz, core, home), place)
        fourth.append(copy)
        if o == 0:

            @pl.when(jnp.logical_not(at_home))
            def _():
                copy.start()

            @pl.when(at_home)
            def _():
                recv4[place] = tot[...]
        else:
            copy.start()
    for xx in range(XN):
        for q in range(per):
            k = xx * per + q
            copy = copy_to(tot, recv4.at[k], 8, 0, sibling, k)

            @pl.when(jnp.logical_not((x == xx) & (z == x * per + q)))
            def _():
                copy.wait_recv()

    send5[...] = recv4[...].reshape(XN * block, channels).astype(BF)
    fifth = send(send5, recv5, 9, 0, sibling)
    rows_n = YN * OWN * GROUP
    cols_n = GROUP * block
    half_n = XN * block
    block_owner = owners_row[:, :block]
    for b in range(1, XN):
        block_owner = jnp.where(x == b, owners_row[:, b * block : (b + 1) * block], block_owner)
    block_owner = jnp.concatenate([block_owner.astype(F32)] * GROUP, axis=1)
    r = iota((rows_n, cols_n), 0)
    c = iota((rows_n, cols_n), 1)
    wanted_slot = lax.rem(lax.div(r, GROUP), OWN)
    wanted = ((lax.div(r, OWN * GROUP) * ZN + z) * CN + core) * OWN + wanted_slot
    c_core = jnp.where(c < half_n, core, 1 - core)
    c_group = lax.div(lax.rem(c, half_n), block) * CN + c_core
    hit = (block_owner == wanted.astype(F32)) & (lax.rem(r, GROUP) == c_group)
    hit = hit.astype(BF)
    fifth.wait_recv()

    sums = jnp.concatenate([send5[...], recv5[...]], axis=0)
    send6[...] = dot(hit, sums).astype(BF).reshape(send6.shape)
    sixth = [
        send(send6.at[yy], recv6.at[y], 10, o, device(yy, z, core, x)) for o, yy in enumerate(ys)
    ]
    recv6[y] = send6[y]
    for copy in sixth:
        copy.wait_recv()

    held = recv6[...].astype(F32)
    taps = YN * GROUP
    table = jnp.concatenate(
        [held[:, s * GROUP : (s + 1) * GROUP].reshape(taps, channels) for s in range(OWN)], axis=0
    )
    turned[...] = table.T
    even = turned[pl.ds(0, channels // 2, stride=2), :]
    odd = turned[pl.ds(1, channels // 2, stride=2), :]
    low_lanes = iota(even.shape, 1) < taps
    slot0 = jnp.where(low_lanes, even, pltpu.roll(odd, taps, 1))
    slot1 = jnp.where(low_lanes, pltpu.roll(even, taps, 1), odd)
    for q in range(channels // 2):
        panels_out[:, q * 128 : (q + 1) * 128] = jnp.concatenate(
            [slot0[q : q + 1], slot1[q : q + 1]], axis=0
        )

    for copy in started:
        copy.wait_send()
    for o, copy in enumerate(fourth):
        if o == 0:

            @pl.when(jnp.logical_not(at_home))
            def _():
                copy.wait_send()
        else:
            copy.wait_send()


def finish(codes_in, panels_in, codes_out, panels_out):
    codes_out[...] = codes_in[...]
    panels_out[...] = panels_in[...]


def body(
    recording,
    spatial_maps,
    temporal_atoms,
    codes_init,
    step_sizes,
    thresholds,
    active_ids,
    active_counts,
    owner_slots,
):
    atoms, taps = temporal_atoms.shape
    channels, length = recording.shape
    slots = active_ids.shape[1]
    width = length + 2 * HALO
    block, part = atoms // XN, atoms // ZN
    shapes = (
        jax.ShapeDtypeStruct((atoms, length), F32),
        jax.ShapeDtypeStruct((OWN, channels * taps), F32),
    )
    results = pl.pallas_call(
        kernel,
        out_shape=shapes,
        in_specs=[HBM] * 9,
        out_specs=(VMEM, VMEM),
        scratch_shapes=[
            pltpu.VMEM((channels, length), BF),
            pltpu.VMEM((atoms, channels), BF),
            pltpu.VMEM((atoms, taps), F32),
            pltpu.VMEM((1, atoms), F32),
            pltpu.VMEM((1, atoms), F32),
            pltpu.VMEM((1, slots), jnp.int32),
            pltpu.VMEM((1, 1), jnp.int32),
            pltpu.VMEM((1, atoms), jnp.int32),
            pltpu.VMEM((atoms, width), F32),
            pltpu.VMEM((atoms, width), F32),
            pltpu.VMEM((channels, 128), BF),
            pltpu.VMEM((8, GROUP * slots), F32),
            pltpu.VMEM((GROUP - 1, 8, GROUP * slots), F32),
            pltpu.VMEM((GROUP, YN, slots, channels), BF),
            pltpu.VMEM((YN, GROUP, slots, channels), BF),
            pltpu.VMEM((YN, atoms, channels), BF),
            pltpu.VMEM((YN - 1, atoms, channels), BF),
            pltpu.VMEM((atoms, channels), F32),
            pltpu.VMEM((ZN - 1, part, channels), F32),
            pltpu.VMEM((part, channels), F32),
            pltpu.VMEM((XN * block // part, part, channels), F32),
            pltpu.VMEM((XN * block, channels), BF),
            pltpu.VMEM((XN * block, channels), BF),
            pltpu.VMEM((YN, OWN * GROUP, channels), BF),
            pltpu.VMEM((YN, OWN * GROUP, channels), BF),
            pltpu.VMEM((channels, OWN * taps), F32),
            pltpu.SemaphoreType.DMA((9,)),
            pltpu.SemaphoreType.DMA((11, 8)),
            pltpu.SemaphoreType.DMA((11, 8)),
        ],
        compiler_params=pltpu.CompilerParams(
            collective_id=0, has_side_effects=True, vmem_limit_bytes=56 << 20
        ),
        name="codes_and_panels",
    )(
        recording,
        spatial_maps,
        temporal_atoms,
        codes_init,
        step_sizes.reshape(1, atoms),
        thresholds.reshape(1, atoms),
        active_ids,
        active_counts.reshape(1, 1),
        owner_slots.reshape(1, atoms),
    )
    return pl.pallas_call(
        finish,
        out_shape=shapes,
        in_specs=[VMEM] * 2,
        out_specs=(VMEM, VMEM),
        name="finish",
    )(*results)


def solution(mesh):
    in_specs = (
        P(None, ("tm", "grp")),
        P(),
        P(),
        P(None, ("tm", "grp")),
        P(),
        P(),
        P(("tm", "grp"), None),
        P(("tm", "grp")),
        P(),
    )
    out_specs = (P(None, ("tm", "grp")), P(("tm", "grp"), None))
    return jax.shard_map(body, mesh=mesh, in_specs=in_specs, out_specs=out_specs, check_vma=False)
```

```python
import functools

import jax
import jax.numpy as jnp
from jax import lax
from jax.experimental import pallas as pl
from jax.experimental.pallas import tpu as pltpu
from jax.sharding import PartitionSpec as P

OWN = 2
XN, YN, ZN, CN = 4, 8, 8, 2
GROUP = XN * CN
HALO = 256
BF = jnp.bfloat16
F32 = jnp.float32
MESH = pl.DeviceIdType.MESH
HBM = pl.BlockSpec(memory_space=pl.ANY)
VMEM = pl.BlockSpec(memory_space=pltpu.VMEM)


def dot(a, b, dims=((1,), (0,))):
    return lax.dot_general(a, b, (dims, ((), ())), preferred_element_type=F32)


def split(v):
    high = v.astype(BF)
    return high, (v - high.astype(F32)).astype(BF)


def iota(shape, dim):
    return lax.broadcasted_iota(jnp.int32, shape, dim)


def to_column(row):
    n = row.shape[1]
    eye = iota((n, n), 0) == iota((n, n), 1)
    return jnp.sum(jnp.where(eye, jnp.broadcast_to(row, (n, n)), 0.0), axis=1, keepdims=True)


def kernel(
    rec_hbm, maps_hbm, waves_hbm, codes_hbm, step_hbm, thresh_hbm, ids_hbm, counts_hbm, owners_hbm,
    codes_out, panels_out,
    rec, maps, waves, step_row, thresh_row, ids_row, counts_row, owners_row,
    xb, pb, rech, tags, tagr, chunk, recv1, send2, recv2, tot, recv4, send5, recv5,
    send6, recv6, turned, in_sem, send_sem, recv_sem, plane_send, plane_recv,
):
    slots = ids_row.shape[1]
    channels, length = rec.shape
    atoms = maps.shape[0]
    block = atoms // XN
    part = atoms // ZN
    n_tm, n_grp = lax.axis_size("tm"), lax.axis_size("grp")
    shards = n_tm * n_grp
    tm = lax.axis_index("tm")
    x = lax.axis_index("grp")
    core = lax.rem(tm, CN)
    z = lax.rem(lax.div(tm, CN), ZN)
    y = lax.div(tm, CN * ZN)
    me = x * CN + core
    shard = tm * n_grp + x

    def device(yy, zz, cc, xx):
        return ((yy * ZN + zz) * CN + cc, xx)

    right, left = lax.rem(shard + 1, shards), lax.rem(shard + shards - 1, shards)
    right_id = (lax.div(right, n_grp), lax.rem(right, n_grp))
    left_id = (lax.div(left, n_grp), lax.rem(left, n_grp))
    pairs = []
    for o in range(1, GROUP):
        xx, cc = lax.rem(x + o // CN, XN), lax.rem(core + o % CN, CN)
        pairs.append((xx * CN + cc, device(y, z, cc, xx)))
    sibling = device(y, z, 1 - core, x)
    ys = [lax.rem(y + o, YN) for o in range(1, YN)]
    plane = []
    for o in range(1, YN * ZN):
        plane.append(device(lax.rem(y + o // ZN, YN), lax.rem(z + o % ZN, ZN), core, x))
    home = lax.div(z * part, block)
    per = block // part
    at_home = x == home

    barrier = pltpu.get_barrier_semaphore()

    def greet(target):
        pl.semaphore_signal(barrier, inc=1, device_id=target, device_id_type=MESH)

    partners = (
        [left_id, right_id]
        + [p for _, p in pairs]
        + plane
    )
    for partner in partners:
        greet(partner)
    for xx in range(XN):
        for q in range(per):
            zz = x * per + q

            @pl.when(jnp.logical_not((x == xx) & (z == zz)))
            def _():
                greet(device(y, zz, core, xx))

    loads = [
        pltpu.make_async_copy(src, dst, in_sem.at[i])
        for i, (src, dst) in enumerate(
            [
                (codes_hbm, xb.at[:, pl.ds(HALO, length)]),
                (rec_hbm, rec),
                (maps_hbm, maps),
                (waves_hbm, waves),
                (step_hbm, step_row),
                (thresh_hbm, thresh_row),
                (ids_hbm, ids_row),
                (counts_hbm, counts_row),
                (owners_hbm, owners_row),
            ]
        )
    ]
    for load in loads:
        load.start()

    started = []

    def copy_to(src, dst, stage, index, target, recv_index=None):
        return pltpu.make_async_remote_copy(
            src_ref=src,
            dst_ref=dst,
            send_sem=send_sem.at[stage, index],
            recv_sem=recv_sem.at[stage, index if recv_index is None else recv_index],
            device_id=target,
            device_id_type=MESH,
        )

    def send(*args):
        copy = copy_to(*args)
        copy.start()
        started.append(copy)
        return copy

    end = HALO + length
    width = end + HALO
    pl.semaphore_wait(barrier, len(partners) + ZN - jnp.where(at_home, 1, 0))
    halo = [
        send(codes_hbm.at[:, pl.ds(0, HALO)], xb.at[:, pl.ds(end, HALO)], 0, 0, left_id),
        send(codes_hbm.at[:, pl.ds(length - HALO, HALO)], xb.at[:, pl.ds(0, HALO)], 0, 1, right_id),
    ]
    for load in loads:
        load.wait()
    pb[:, HALO:end] = dot(maps[...], rec[...])
    halo += [
        send(pb.at[:, pl.ds(HALO, HALO)], pb.at[:, pl.ds(end, HALO)], 0, 2, left_id),
        send(pb.at[:, pl.ds(end - 128, 128)], pb.at[:, pl.ds(128, 128)], 0, 3, right_id),
    ]
    pb[:, :128] = jnp.zeros((atoms, 128), F32)

    live = iota((1, slots), 1) < jnp.broadcast_to(counts_row[...], (1, slots))
    ids = jnp.where(live, ids_row[...].astype(F32), -1.0)
    tags[...] = jnp.broadcast_to(jnp.concatenate([ids] * GROUP, axis=1), tags.shape)
    select = (iota((slots, atoms), 1).astype(F32) == to_column(ids)).astype(BF)

    half = atoms // 2
    lanes = 8 * half
    pick_lag = iota((64, 8 * lanes), 1)
    pick_lag = lax.div(pick_lag, lanes) * 8 + lax.div(lax.rem(pick_lag, lanes), half)
    pick_lag = (pick_lag == iota((64, 8 * lanes), 0)).astype(BF)
    same = (iota((half, lanes), 0) == lax.rem(iota((half, lanes), 1), half)).astype(F32)
    spread = [dot(v, pick_lag) for v in split(waves[...])]
    filters = []
    for g in range(2):
        high, low = [
            jnp.concatenate(
                [
                    (v[g * half : (g + 1) * half, i * lanes : (i + 1) * lanes] * same).astype(BF)
                    for i in range(8)
                ],
                axis=0,
            )
            for v in spread
        ]
        filters.append(jnp.concatenate([high, high, low], axis=1))
    high, low = split(dot(maps[...], maps[...], ((1,), (1,))))
    gram = jnp.concatenate([high, high, low], axis=1)
    step = to_column(step_row[...])
    thresh = to_column(thresh_row[...])

    def depthwise(v, sign):
        n = v.shape[1]
        rolled = [
            [u if j == 0 else pltpu.roll(u, (sign * j) % n, 1) for j in range(8)] for u in split(v)
        ]
        groups = []
        for g in range(2):
            high, low = [
                jnp.concatenate([u[g * half : (g + 1) * half] for u in us], axis=0) for us in rolled
            ]
            w = dot(filters[g], jnp.concatenate([high, low, high], axis=0))
            total = w[:half]
            for i in range(1, 8):
                total = total + pltpu.roll(w[i * half : (i + 1) * half], (sign * 8 * i) % n, 1)
            groups.append(total)
        return jnp.concatenate(groups, axis=0)

    for copy in halo[:2]:
        copy.wait_recv()
    first = jnp.where(shard == 0, HALO, 0)
    last = jnp.where(shard == shards - 1, end, width + HALO)

    def column(start, stop):
        return iota((atoms, stop - start), 1) + start

    windows = [((128, width), (128, 1408)), ((128, 1408), (128, 1408)), ((HALO, 1408), (HALO, end))]
    v = jnp.where(column(0, width) < first, 0.0, xb[...])
    v_from = 0
    for (r_from, r_to), (c_from, c_to) in windows:
        synthesis = depthwise(v, 1)[:, r_from - v_from : r_to - v_from]
        high, low = split(synthesis)
        mixed = dot(gram, jnp.concatenate([high, low, high], axis=0))
        if v_from == 0:
            for copy in halo[2:]:
                copy.wait_recv()
            more = [send(rec.at[:, pl.ds(0, 128)], rech, 0, 4, left_id)]
            tag_copies = [send(tags, tagr.at[o], 1, o, p) for o, (_, p) in enumerate(pairs)]
        r = pb[:, r_from:r_to] - mixed
        r = jnp.where(column(r_from, r_to) < last, r, 0.0)
        g = depthwise(r, -1)[:, c_from - r_from : c_to - r_from]
        v = v[:, c_from - v_from : c_to - v_from]
        v = jnp.maximum(v + step * g - thresh, 0.0)
        v = jnp.where(column(c_from, c_to) < first, 0.0, v)
        v_from = c_from
    codes_out[...] = v

    picked = dot(select, v.astype(BF)).astype(BF)
    picked = jnp.concatenate([picked, jnp.zeros((slots, 128), BF)], axis=1)
    shifted = jnp.concatenate(
        [picked if j == 0 else pltpu.roll(picked, j, 1) for j in range(16)], axis=0
    )
    more[0].wait_recv()
    after = jnp.where(shard == shards - 1, jnp.zeros_like(rech), rech[...])
    window = jnp.concatenate([rec[...], after], axis=1)
    n = length + 128
    pieces = YN // 2
    order = [lax.rem(lax.div(y, 2) + p + 1, pieces) for p in range(pieces)]
    firsts = []
    for p in range(pieces):
        i = order[p]
        moved = pltpu.roll(window, lax.rem(n - 16 * i, n), 1)
        panel = dot(shifted, moved, ((1,), (1,)))
        panel = (panel * float(length) ** -0.5).astype(BF)
        for j in range(16):
            chunk[j % 8, 2 * i + j // 8] = panel[j * slots : (j + 1) * slots]
        rows = pl.ds(2 * i, 2)
        firsts.append(
            [
                send(chunk.at[d, rows], recv1.at[rows, me], 2 + p, o, target)
                for o, (d, target) in enumerate(pairs)
            ]
        )
        recv1[rows, me] = chunk[me, rows]

    wide = recv2.shape[2]

    def part_of(t, zz):
        rows = pl.multiple_of(lax.div(zz, per) * block, block)
        cols = pl.multiple_of(lax.rem(zz, per) * (channels - wide), 128)
        return send2.at[t, pl.ds(rows, block), pl.ds(cols, wide)]

    def plane_copy(src, o, target):
        return pltpu.make_async_remote_copy(
            src_ref=src,
            dst_ref=recv2.at[o - 1],
            send_sem=plane_send.at[o - 1],
            recv_sem=plane_recv.at[o - 1],
            device_id=target,
            device_id_type=MESH,
        )

    for copy in tag_copies:
        copy.wait_recv()
    lane = iota((1, GROUP * slots), 1)
    source = lax.div(lane, slots)
    row = jnp.where(source == me, tags[:1], -1.0)
    for o in range(1, GROUP):
        frm = lax.rem(x - o // CN + XN, XN) * CN + lax.rem(core - o % CN + CN, CN)
        row = jnp.where(source == frm, tagr[o - 1, :1], row)
    expand = (iota((atoms, GROUP * slots), 0).astype(F32) == row).astype(BF)
    for p in range(pieces):
        for copy in firsts[p]:
            copy.wait_recv()
        for q in range(2):
            t = 2 * order[p] + q
            terms = recv1[t].reshape(GROUP * slots, channels)
            send2[t] = dot(expand, terms).astype(BF)
            for k in range(ZN):
                zz = lax.rem(z + k, ZN)
                o = lax.rem(t - y + YN, YN) * ZN + k

                @pl.when(o != 0)
                def _():
                    plane_copy(part_of(t, zz), o, device(t, zz, core, x)).start()

    acc = part_of(y, z)[...].astype(F32)
    for o in range(1, YN * ZN):
        copy = plane_copy(part_of(0, 0), o, plane[o - 1])
        copy.wait_recv()
        started.append(copy)
        acc = acc + recv2[o - 1].astype(F32)
    tot[...] = acc.astype(BF)

    place = x * per + lax.rem(z, per)
    fourth = []
    for o in range(ZN):
        zz = lax.rem(z + o, ZN)
        copy = copy_to(tot, recv4.at[place], 8, o, device(y, zz, core, home), place)
        fourth.append(copy)
        if o == 0:

            @pl.when(jnp.logical_not(at_home))
            def _():
                copy.start()

            @pl.when(at_home)
            def _():
                recv4[place] = tot[...]
        else:
            copy.start()
    for xx in range(XN):
        for q in range(per):
            k = xx * per + q
            copy = copy_to(tot, recv4.at[k], 8, 0, sibling, k)

            @pl.when(jnp.logical_not((x == xx) & (z == x * per + q)))
            def _():
                copy.wait_recv()

    for xx in range(XN):
        send5[xx * block : (xx + 1) * block, :wide] = recv4[per * xx]
        send5[xx * block : (xx + 1) * block, wide:] = recv4[per * xx + 1, :, 2 * wide - channels :]
    fifth = send(send5, recv5, 9, 0, sibling)
    rows_n = YN * OWN * GROUP
    cols_n = GROUP * block
    half_n = XN * block
    block_owner = owners_row[:, :block]
    for b in range(1, XN):
        block_owner = jnp.where(x == b, owners_row[:, b * block : (b + 1) * block], block_owner)
    block_owner = jnp.concatenate([block_owner.astype(F32)] * GROUP, axis=1)
    r = iota((rows_n, cols_n), 0)
    c = iota((rows_n, cols_n), 1)
    wanted_slot = lax.rem(lax.div(r, GROUP), OWN)
    wanted = ((lax.div(r, OWN * GROUP) * ZN + z) * CN + core) * OWN + wanted_slot
    c_core = jnp.where(c < half_n, core, 1 - core)
    c_group = lax.div(lax.rem(c, half_n), block) * CN + c_core
    hit = (block_owner == wanted.astype(F32)) & (lax.rem(r, GROUP) == c_group)
    hit = hit.astype(BF)
    fifth.wait_recv()

    sums = jnp.concatenate([send5[...], recv5[...]], axis=0)
    send6[...] = dot(hit, sums).astype(BF).reshape(send6.shape)
    sixth = [
        send(send6.at[yy], recv6.at[y], 10, o, device(yy, z, core, x)) for o, yy in enumerate(ys)
    ]
    recv6[y] = send6[y]
    for copy in sixth:
        copy.wait_recv()

    held = recv6[...].astype(F32)
    taps = YN * GROUP
    table = jnp.concatenate(
        [held[:, s * GROUP : (s + 1) * GROUP].reshape(taps, channels) for s in range(OWN)], axis=0
    )
    turned[...] = table.T
    even = turned[pl.ds(0, channels // 2, stride=2), :]
    odd = turned[pl.ds(1, channels // 2, stride=2), :]
    low_lanes = iota(even.shape, 1) < taps
    slot0 = jnp.where(low_lanes, even, pltpu.roll(odd, taps, 1))
    slot1 = jnp.where(low_lanes, pltpu.roll(even, taps, 1), odd)
    for q in range(channels // 2):
        panels_out[:, q * 128 : (q + 1) * 128] = jnp.concatenate(
            [slot0[q : q + 1], slot1[q : q + 1]], axis=0
        )

    for copy in started:
        copy.wait_send()
    for o, copy in enumerate(fourth):
        if o == 0:

            @pl.when(jnp.logical_not(at_home))
            def _():
                copy.wait_send()
        else:
            copy.wait_send()


def finish(codes_in, panels_in, codes_out, panels_out):
    codes_out[...] = codes_in[...]
    panels_out[...] = panels_in[...]


def body(
    recording,
    spatial_maps,
    temporal_atoms,
    codes_init,
    step_sizes,
    thresholds,
    active_ids,
    active_counts,
    owner_slots,
):
    atoms, taps = temporal_atoms.shape
    channels, length = recording.shape
    slots = active_ids.shape[1]
    width = length + 2 * HALO
    block, part = atoms // XN, atoms // ZN
    shapes = (
        jax.ShapeDtypeStruct((atoms, length), F32),
        jax.ShapeDtypeStruct((OWN, channels * taps), F32),
    )
    results = pl.pallas_call(
        kernel,
        out_shape=shapes,
        in_specs=[HBM] * 9,
        out_specs=(VMEM, VMEM),
        scratch_shapes=[
            pltpu.VMEM((channels, length), BF),
            pltpu.VMEM((atoms, channels), BF),
            pltpu.VMEM((atoms, taps), F32),
            pltpu.VMEM((1, atoms), F32),
            pltpu.VMEM((1, atoms), F32),
            pltpu.VMEM((1, slots), jnp.int32),
            pltpu.VMEM((1, 1), jnp.int32),
            pltpu.VMEM((1, atoms), jnp.int32),
            pltpu.VMEM((atoms, width), F32),
            pltpu.VMEM((atoms, width), F32),
            pltpu.VMEM((channels, 128), BF),
            pltpu.VMEM((8, GROUP * slots), F32),
            pltpu.VMEM((GROUP - 1, 8, GROUP * slots), F32),
            pltpu.VMEM((GROUP, YN, slots, channels), BF),
            pltpu.VMEM((YN, GROUP, slots, channels), BF),
            pltpu.VMEM((YN, atoms, channels), BF),
            pltpu.VMEM((YN * ZN - 1, block, 256), BF),
            pltpu.VMEM((block, 256), BF),
            pltpu.VMEM((XN * block // part, block, 256), BF),
            pltpu.VMEM((XN * block, channels), BF),
            pltpu.VMEM((XN * block, channels), BF),
            pltpu.VMEM((YN, OWN * GROUP, channels), BF),
            pltpu.VMEM((YN, OWN * GROUP, channels), BF),
            pltpu.VMEM((channels, OWN * taps), F32),
            pltpu.SemaphoreType.DMA((9,)),
            pltpu.SemaphoreType.DMA((11, 8)),
            pltpu.SemaphoreType.DMA((11, 8)),
            pltpu.SemaphoreType.DMA((YN * ZN - 1,)),
            pltpu.SemaphoreType.DMA((YN * ZN - 1,)),
        ],
        compiler_params=pltpu.CompilerParams(
            collective_id=0, has_side_effects=True, vmem_limit_bytes=56 << 20
        ),
        name="codes_and_panels",
    )(
        recording,
        spatial_maps,
        temporal_atoms,
        codes_init,
        step_sizes.reshape(1, atoms),
        thresholds.reshape(1, atoms),
        active_ids,
        active_counts.reshape(1, 1),
        owner_slots.reshape(1, atoms),
    )
    return pl.pallas_call(
        finish,
        out_shape=shapes,
        in_specs=[VMEM] * 2,
        out_specs=(VMEM, VMEM),
        name="finish",
    )(*results)


def solution(mesh):
    in_specs = (
        P(None, ("tm", "grp")),
        P(),
        P(),
        P(None, ("tm", "grp")),
        P(),
        P(),
        P(("tm", "grp"), None),
        P(("tm", "grp")),
        P(),
    )
    out_specs = (P(None, ("tm", "grp")), P(("tm", "grp"), None))
    return jax.shard_map(body, mesh=mesh, in_specs=in_specs, out_specs=out_specs, check_vma=False)
```

```python
import functools

import jax
import jax.numpy as jnp
from jax import lax
from jax.experimental import pallas as pl
from jax.experimental.pallas import tpu as pltpu
from jax.sharding import PartitionSpec as P

OWN = 2
XN, YN, ZN, CN = 4, 8, 8, 2
GROUP = XN * CN
HALO = 256
BF = jnp.bfloat16
F32 = jnp.float32
MESH = pl.DeviceIdType.MESH
HBM = pl.BlockSpec(memory_space=pl.ANY)
VMEM = pl.BlockSpec(memory_space=pltpu.VMEM)


def dot(a, b, dims=((1,), (0,))):
    return lax.dot_general(a, b, (dims, ((), ())), preferred_element_type=F32)


def split(v):
    high = v.astype(BF)
    return high, (v - high.astype(F32)).astype(BF)


def iota(shape, dim):
    return lax.broadcasted_iota(jnp.int32, shape, dim)


def over(v, size):
    return v >> (size.bit_length() - 1)


def within(v, size):
    return v & (size - 1)


def to_column(row):
    n = row.shape[1]
    eye = iota((n, n), 0) == iota((n, n), 1)
    return jnp.sum(jnp.where(eye, jnp.broadcast_to(row, (n, n)), 0.0), axis=1, keepdims=True)


def kernel(
    rec_hbm, maps_hbm, waves_hbm, codes_hbm, step_hbm, thresh_hbm, ids_hbm, counts_hbm, owners_hbm,
    codes_out, panels_out,
    rec, maps, waves, step_row, thresh_row, ids_row, counts_row, owners_row,
    xb, pb, rech, tags, tagr, chunk, recv1, send2, recv2, send3, recv3, tot, recv4, send5, recv5,
    send6, recv6, turned, in_sem, send_sem, recv_sem,
):
    slots = ids_row.shape[1]
    channels, length = rec.shape
    atoms = maps.shape[0]
    block = atoms // XN
    part = atoms // ZN
    n_tm, n_grp = lax.axis_size("tm"), lax.axis_size("grp")
    shards = n_tm * n_grp
    tm = lax.axis_index("tm")
    x = lax.axis_index("grp")
    core = lax.rem(tm, CN)
    z = lax.rem(lax.div(tm, CN), ZN)
    y = lax.div(tm, CN * ZN)
    me = x * CN + core
    shard = tm * n_grp + x

    def device(yy, zz, cc, xx):
        return ((yy * ZN + zz) * CN + cc, xx)

    right, left = lax.rem(shard + 1, shards), lax.rem(shard + shards - 1, shards)
    right_id = (lax.div(right, n_grp), lax.rem(right, n_grp))
    left_id = (lax.div(left, n_grp), lax.rem(left, n_grp))
    pairs = []
    for o in range(1, GROUP):
        xx, cc = lax.rem(x + o // CN, XN), lax.rem(core + o % CN, CN)
        pairs.append((xx * CN + cc, device(y, z, cc, xx)))
    sibling = device(y, z, 1 - core, x)
    ys = [lax.rem(y + o, YN) for o in range(1, YN)]
    zs = [lax.rem(z + o, ZN) for o in range(1, ZN)]
    home = lax.div(z * part, block)
    per = block // part
    at_home = x == home

    barrier = pltpu.get_barrier_semaphore()

    def greet(target):
        pl.semaphore_signal(barrier, inc=1, device_id=target, device_id_type=MESH)

    partners = (
        [left_id, right_id]
        + [p for _, p in pairs]
        + [device(yy, z, core, x) for yy in ys]
        + [device(y, zz, core, x) for zz in zs]
    )
    for partner in partners:
        greet(partner)
    for xx in range(XN):
        for q in range(per):
            zz = x * per + q

            @pl.when(jnp.logical_not((x == xx) & (z == zz)))
            def _():
                greet(device(y, zz, core, xx))

    loads = [
        pltpu.make_async_copy(src, dst, in_sem.at[i])
        for i, (src, dst) in enumerate(
            [
                (codes_hbm, xb.at[:, pl.ds(HALO, length)]),
                (rec_hbm, rec),
                (maps_hbm, maps),
                (waves_hbm, waves),
                (step_hbm, step_row),
                (thresh_hbm, thresh_row),
                (ids_hbm, ids_row),
                (counts_hbm, counts_row),
                (owners_hbm, owners_row),
            ]
        )
    ]
    for load in loads:
        load.start()

    started = []

    def copy_to(src, dst, stage, index, target, recv_index=None):
        return pltpu.make_async_remote_copy(
            src_ref=src,
            dst_ref=dst,
            send_sem=send_sem.at[stage, index],
            recv_sem=recv_sem.at[stage, index if recv_index is None else recv_index],
            device_id=target,
            device_id_type=MESH,
        )

    def send(*args):
        copy = copy_to(*args)
        copy.start()
        started.append(copy)
        return copy

    end = HALO + length
    width = end + HALO
    pl.semaphore_wait(barrier, len(partners) + ZN - jnp.where(at_home, 1, 0))
    halo = [
        send(codes_hbm.at[:, pl.ds(0, HALO)], xb.at[:, pl.ds(end, HALO)], 0, 0, left_id),
        send(codes_hbm.at[:, pl.ds(length - HALO, HALO)], xb.at[:, pl.ds(0, HALO)], 0, 1, right_id),
    ]
    for load in loads:
        load.wait()
    pb[:, HALO:end] = dot(maps[...], rec[...])
    halo += [
        send(pb.at[:, pl.ds(HALO, HALO)], pb.at[:, pl.ds(end, HALO)], 0, 2, left_id),
        send(pb.at[:, pl.ds(end - 128, 128)], pb.at[:, pl.ds(128, 128)], 0, 3, right_id),
    ]
    pb[:, :128] = jnp.zeros((atoms, 128), F32)

    live = iota((1, slots), 1) < jnp.broadcast_to(counts_row[...], (1, slots))
    ids = jnp.where(live, ids_row[...].astype(F32), -1.0)
    tags[...] = jnp.broadcast_to(jnp.concatenate([ids] * GROUP, axis=1), tags.shape)
    select = (iota((slots, atoms), 1).astype(F32) == to_column(ids)).astype(BF)

    half = atoms // 2
    lanes = 8 * half
    pick_lag = iota((64, 8 * lanes), 1)
    pick_lag = over(pick_lag, lanes) * 8 + over(within(pick_lag, lanes), half)
    pick_lag = (pick_lag == iota((64, 8 * lanes), 0)).astype(BF)
    same = (iota((half, lanes), 0) == within(iota((half, lanes), 1), half)).astype(F32)
    spread = [dot(v, pick_lag) for v in split(waves[...])]
    filters = []
    for g in range(2):
        high, low = [
            jnp.concatenate(
                [
                    (v[g * half : (g + 1) * half, i * lanes : (i + 1) * lanes] * same).astype(BF)
                    for i in range(8)
                ],
                axis=0,
            )
            for v in spread
        ]
        filters.append(jnp.concatenate([high, high, low], axis=1))
    high, low = split(dot(maps[...], maps[...], ((1,), (1,))))
    gram = jnp.concatenate([high, high, low], axis=1)
    step = to_column(step_row[...])
    thresh = to_column(thresh_row[...])

    def depthwise(v, sign):
        n = v.shape[1]
        rolled = [
            [u if j == 0 else pltpu.roll(u, (sign * j) % n, 1) for j in range(8)] for u in split(v)
        ]
        groups = []
        for g in range(2):
            high, low = [
                jnp.concatenate([u[g * half : (g + 1) * half] for u in us], axis=0) for us in rolled
            ]
            w = dot(filters[g], jnp.concatenate([high, low, high], axis=0))
            total = w[:half]
            for i in range(1, 8):
                total = total + pltpu.roll(w[i * half : (i + 1) * half], (sign * 8 * i) % n, 1)
            groups.append(total)
        return jnp.concatenate(groups, axis=0)

    for copy in halo[:2]:
        copy.wait_recv()
    first = jnp.where(shard == 0, HALO, 0)
    last = jnp.where(shard == shards - 1, end, width + HALO)

    def column(start, stop):
        return iota((atoms, stop - start), 1) + start

    windows = [((128, width), (128, 1408)), ((128, 1408), (128, 1408)), ((HALO, 1408), (HALO, end))]
    v = jnp.where(column(0, width) < first, 0.0, xb[...])
    v_from = 0
    for (r_from, r_to), (c_from, c_to) in windows:
        synthesis = depthwise(v, 1)[:, r_from - v_from : r_to - v_from]
        high, low = split(synthesis)
        mixed = dot(gram, jnp.concatenate([high, low, high], axis=0))
        if v_from == 0:
            for copy in halo[2:]:
                copy.wait_recv()
            more = [send(rec.at[:, pl.ds(0, 128)], rech, 0, 4, left_id)]
            tag_copies = [send(tags, tagr.at[o], 1, o, p) for o, (_, p) in enumerate(pairs)]
        r = pb[:, r_from:r_to] - mixed
        r = jnp.where(column(r_from, r_to) < last, r, 0.0)
        g = depthwise(r, -1)[:, c_from - r_from : c_to - r_from]
        v = v[:, c_from - v_from : c_to - v_from]
        v = jnp.maximum(v + step * g - thresh, 0.0)
        v = jnp.where(column(c_from, c_to) < first, 0.0, v)
        v_from = c_from

    picked = dot(select, v.astype(BF)).astype(BF)
    picked = jnp.concatenate([picked, jnp.zeros((slots, 128), BF)], axis=1)
    shifted = jnp.concatenate(
        [picked if j == 0 else pltpu.roll(picked, j, 1) for j in range(16)], axis=0
    )
    more[0].wait_recv()
    after = jnp.where(shard == shards - 1, jnp.zeros_like(rech), rech[...])
    window = jnp.concatenate([rec[...], after], axis=1)
    n = length + 128
    pieces = YN // 2
    order = [lax.rem(lax.div(y, 2) + p + 1, pieces) for p in range(pieces)]
    firsts = []
    for p in range(pieces):
        i = order[p]
        moved = pltpu.roll(window, lax.rem(n - 16 * i, n), 1)
        panel = dot(shifted, moved, ((1,), (1,)))
        panel = (panel * float(length) ** -0.5).astype(BF)
        for j in range(16):
            chunk[j % 8, 2 * i + j // 8] = panel[j * slots : (j + 1) * slots]
        rows = pl.ds(2 * i, 2)
        firsts.append(
            [
                send(chunk.at[d, rows], recv1.at[rows, me], 2 + p, o, target)
                for o, (d, target) in enumerate(pairs)
            ]
        )
        recv1[rows, me] = chunk[me, rows]

    codes_out[...] = v

    for copy in tag_copies:
        copy.wait_recv()
    lane = iota((1, GROUP * slots), 1)
    source = over(lane, slots)
    row = jnp.where(source == me, tags[:1], -1.0)
    for o in range(1, GROUP):
        frm = lax.rem(x - o // CN + XN, XN) * CN + lax.rem(core - o % CN + CN, CN)
        row = jnp.where(source == frm, tagr[o - 1, :1], row)
    expand = (iota((atoms, GROUP * slots), 0).astype(F32) == row).astype(BF)
    for p in range(pieces):
        for copy in firsts[p]:
            copy.wait_recv()
        for q in range(2):
            t = 2 * order[p] + q
            terms = recv1[t].reshape(GROUP * slots, channels)
            send2[t] = dot(expand, terms).astype(BF)
            o = lax.rem(t - y + YN, YN)

            @pl.when(o != 0)
            def _():
                copy_to(send2.at[t], recv2.at[o - 1], 6, o - 1, device(t, z, core, x)).start()

    acc = send2[y].astype(F32)
    for o in range(YN - 1):
        copy = copy_to(send2.at[0], recv2.at[o], 6, o, device(ys[0], z, core, x))
        copy.wait_recv()
        started.append(copy)
        acc = acc + recv2[o].astype(F32)
    send3[...] = acc

    third = [
        send(send3.at[pl.ds(zz * part, part)], recv3.at[o], 7, o, device(y, zz, core, x))
        for o, zz in enumerate(zs)
    ]
    acc = send3[pl.ds(pl.multiple_of(z * part, part), part)]
    for o, copy in enumerate(third):
        copy.wait_recv()
        acc = acc + recv3[o]
    tot[...] = acc

    place = x * per + lax.rem(z, per)
    fourth = []
    for o in range(ZN):
        zz = lax.rem(z + o, ZN)
        copy = copy_to(tot, recv4.at[place], 8, o, device(y, zz, core, home), place)
        fourth.append(copy)
        if o == 0:

            @pl.when(jnp.logical_not(at_home))
            def _():
                copy.start()

            @pl.when(at_home)
            def _():
                recv4[place] = tot[...]
        else:
            copy.start()
    for xx in range(XN):
        for q in range(per):
            k = xx * per + q
            copy = copy_to(tot, recv4.at[k], 8, 0, sibling, k)

            @pl.when(jnp.logical_not((x == xx) & (z == x * per + q)))
            def _():
                copy.wait_recv()

    send5[...] = recv4[...].reshape(XN * block, channels).astype(BF)
    fifth = send(send5, recv5, 9, 0, sibling)
    rows_n = YN * OWN * GROUP
    cols_n = GROUP * block
    half_n = XN * block
    block_owner = owners_row[:, :block]
    for b in range(1, XN):
        block_owner = jnp.where(x == b, owners_row[:, b * block : (b + 1) * block], block_owner)
    block_owner = jnp.concatenate([block_owner.astype(F32)] * GROUP, axis=1)
    r = iota((rows_n, cols_n), 0)
    c = iota((rows_n, cols_n), 1)
    wanted_slot = within(over(r, GROUP), OWN)
    wanted = ((over(r, OWN * GROUP) * ZN + z) * CN + core) * OWN + wanted_slot
    c_core = jnp.where(c < half_n, core, 1 - core)
    c_group = over(within(c, half_n), block) * CN + c_core
    hit = (block_owner == wanted.astype(F32)) & (within(r, GROUP) == c_group)
    hit = hit.astype(BF)
    fifth.wait_recv()

    sums = jnp.concatenate([send5[...], recv5[...]], axis=0)
    send6[...] = dot(hit, sums).astype(BF).reshape(send6.shape)
    sixth = [
        send(send6.at[yy], recv6.at[y], 10, o, device(yy, z, core, x)) for o, yy in enumerate(ys)
    ]
    recv6[y] = send6[y]
    for copy in sixth:
        copy.wait_recv()

    held = recv6[...].astype(F32)
    taps = YN * GROUP
    table = jnp.concatenate(
        [held[:, s * GROUP : (s + 1) * GROUP].reshape(taps, channels) for s in range(OWN)], axis=0
    )
    turned[...] = table.T
    even = turned[pl.ds(0, channels // 2, stride=2), :]
    odd = turned[pl.ds(1, channels // 2, stride=2), :]
    low_lanes = iota(even.shape, 1) < taps
    slot0 = jnp.where(low_lanes, even, pltpu.roll(odd, taps, 1))
    slot1 = jnp.where(low_lanes, pltpu.roll(even, taps, 1), odd)
    for q in range(channels // 2):
        panels_out[:, q * 128 : (q + 1) * 128] = jnp.concatenate(
            [slot0[q : q + 1], slot1[q : q + 1]], axis=0
        )

    for copy in started:
        copy.wait_send()
    for o, copy in enumerate(fourth):
        if o == 0:

            @pl.when(jnp.logical_not(at_home))
            def _():
                copy.wait_send()
        else:
            copy.wait_send()


def finish(codes_in, panels_in, codes_out, panels_out):
    codes_out[...] = codes_in[...]
    panels_out[...] = panels_in[...]


def body(
    recording,
    spatial_maps,
    temporal_atoms,
    codes_init,
    step_sizes,
    thresholds,
    active_ids,
    active_counts,
    owner_slots,
):
    atoms, taps = temporal_atoms.shape
    channels, length = recording.shape
    slots = active_ids.shape[1]
    width = length + 2 * HALO
    block, part = atoms // XN, atoms // ZN
    shapes = (
        jax.ShapeDtypeStruct((atoms, length), F32),
        jax.ShapeDtypeStruct((OWN, channels * taps), F32),
    )
    results = pl.pallas_call(
        kernel,
        out_shape=shapes,
        in_specs=[HBM] * 9,
        out_specs=(VMEM, VMEM),
        scratch_shapes=[
            pltpu.VMEM((channels, length), BF),
            pltpu.VMEM((atoms, channels), BF),
            pltpu.VMEM((atoms, taps), F32),
            pltpu.VMEM((1, atoms), F32),
            pltpu.VMEM((1, atoms), F32),
            pltpu.VMEM((1, slots), jnp.int32),
            pltpu.VMEM((1, 1), jnp.int32),
            pltpu.VMEM((1, atoms), jnp.int32),
            pltpu.VMEM((atoms, width), F32),
            pltpu.VMEM((atoms, width), F32),
            pltpu.VMEM((channels, 128), BF),
            pltpu.VMEM((8, GROUP * slots), F32),
            pltpu.VMEM((GROUP - 1, 8, GROUP * slots), F32),
            pltpu.VMEM((GROUP, YN, slots, channels), BF),
            pltpu.VMEM((YN, GROUP, slots, channels), BF),
            pltpu.VMEM((YN, atoms, channels), BF),
            pltpu.VMEM((YN - 1, atoms, channels), BF),
            pltpu.VMEM((atoms, channels), F32),
            pltpu.VMEM((ZN - 1, part, channels), F32),
            pltpu.VMEM((part, channels), F32),
            pltpu.VMEM((XN * block // part, part, channels), F32),
            pltpu.VMEM((XN * block, channels), BF),
            pltpu.VMEM((XN * block, channels), BF),
            pltpu.VMEM((YN, OWN * GROUP, channels), BF),
            pltpu.VMEM((YN, OWN * GROUP, channels), BF),
            pltpu.VMEM((channels, OWN * taps), F32),
            pltpu.SemaphoreType.DMA((9,)),
            pltpu.SemaphoreType.DMA((11, 8)),
            pltpu.SemaphoreType.DMA((11, 8)),
        ],
        compiler_params=pltpu.CompilerParams(
            collective_id=0, has_side_effects=True, vmem_limit_bytes=56 << 20
        ),
        name="codes_and_panels",
    )(
        recording,
        spatial_maps,
        temporal_atoms,
        codes_init,
        step_sizes.reshape(1, atoms),
        thresholds.reshape(1, atoms),
        active_ids,
        active_counts.reshape(1, 1),
        owner_slots.reshape(1, atoms),
    )
    return pl.pallas_call(
        finish,
        out_shape=shapes,
        in_specs=[VMEM] * 2,
        out_specs=(VMEM, VMEM),
        name="finish",
    )(*results)


def solution(mesh):
    in_specs = (
        P(None, ("tm", "grp")),
        P(),
        P(),
        P(None, ("tm", "grp")),
        P(),
        P(),
        P(("tm", "grp"), None),
        P(("tm", "grp")),
        P(),
    )
    out_specs = (P(None, ("tm", "grp")), P(("tm", "grp"), None))
    return jax.shard_map(body, mesh=mesh, in_specs=in_specs, out_specs=out_specs, check_vma=False)
```

```python
import functools

import jax
import jax.numpy as jnp
from jax import lax
from jax.experimental import pallas as pl
from jax.experimental.pallas import tpu as pltpu
from jax.sharding import PartitionSpec as P

OWN = 2
XN, YN, ZN, CN = 4, 8, 8, 2
GROUP = XN * CN
HALO = 256
BF = jnp.bfloat16
F32 = jnp.float32
MESH = pl.DeviceIdType.MESH
HBM = pl.BlockSpec(memory_space=pl.ANY)
VMEM = pl.BlockSpec(memory_space=pltpu.VMEM)


def dot(a, b, dims=((1,), (0,))):
    return lax.dot_general(a, b, (dims, ((), ())), preferred_element_type=F32)


def split(v):
    high = v.astype(BF)
    return high, (v - high.astype(F32)).astype(BF)


def iota(shape, dim):
    return lax.broadcasted_iota(jnp.int32, shape, dim)


def over(v, size):
    return v >> (size.bit_length() - 1)


def within(v, size):
    return v & (size - 1)


def to_column(row):
    n = row.shape[1]
    eye = iota((n, n), 0) == iota((n, n), 1)
    return jnp.sum(jnp.where(eye, jnp.broadcast_to(row, (n, n)), 0.0), axis=1, keepdims=True)


def kernel(
    rec_hbm, maps_hbm, waves_hbm, codes_hbm, step_hbm, thresh_hbm, ids_hbm, counts_hbm, owners_hbm,
    codes_out, panels_out,
    rec, maps, waves, step_row, thresh_row, ids_row, counts_row, owners_row,
    xb, pb, rech, tags, tagr, chunk, recv1, send2, recv2, send3, recv3, tot, recv4, send5, recv5,
    send6, recv6, turned, in_sem, send_sem, recv_sem,
):
    slots = ids_row.shape[1]
    channels, length = rec.shape
    atoms = maps.shape[0]
    block = atoms // XN
    part = atoms // ZN
    n_tm, n_grp = lax.axis_size("tm"), lax.axis_size("grp")
    shards = n_tm * n_grp
    tm = lax.axis_index("tm")
    x = lax.axis_index("grp")
    core = lax.rem(tm, CN)
    z = lax.rem(lax.div(tm, CN), ZN)
    y = lax.div(tm, CN * ZN)
    me = x * CN + core
    shard = tm * n_grp + x

    def device(yy, zz, cc, xx):
        return ((yy * ZN + zz) * CN + cc, xx)

    right, left = lax.rem(shard + 1, shards), lax.rem(shard + shards - 1, shards)
    right_id = (lax.div(right, n_grp), lax.rem(right, n_grp))
    left_id = (lax.div(left, n_grp), lax.rem(left, n_grp))
    pairs = []
    for o in range(1, GROUP):
        xx, cc = lax.rem(x + o // CN, XN), lax.rem(core + o % CN, CN)
        pairs.append((xx * CN + cc, device(y, z, cc, xx)))
    sibling = device(y, z, 1 - core, x)
    ys = [lax.rem(y + o, YN) for o in range(1, YN)]
    zs = [lax.rem(z + o, ZN) for o in range(1, ZN)]
    home = lax.div(z * part, block)
    per = block // part
    at_home = x == home

    barrier = pltpu.get_barrier_semaphore()

    def greet(target):
        pl.semaphore_signal(barrier, inc=1, device_id=target, device_id_type=MESH)

    partners = (
        [left_id, right_id]
        + [p for _, p in pairs]
        + [device(yy, z, core, x) for yy in ys]
        + [device(y, zz, core, x) for zz in zs]
    )
    for partner in partners:
        greet(partner)
    for xx in range(XN):
        for q in range(per):
            zz = x * per + q

            @pl.when(jnp.logical_not((x == xx) & (z == zz)))
            def _():
                greet(device(y, zz, core, xx))

    loads = [
        pltpu.make_async_copy(src, dst, in_sem.at[i])
        for i, (src, dst) in enumerate(
            [
                (codes_hbm, xb.at[:, pl.ds(HALO, length)]),
                (rec_hbm, rec),
                (maps_hbm, maps),
                (waves_hbm, waves),
                (step_hbm, step_row),
                (thresh_hbm, thresh_row),
                (ids_hbm, ids_row),
                (counts_hbm, counts_row),
                (owners_hbm, owners_row),
            ]
        )
    ]
    for load in loads:
        load.start()

    started = []

    def copy_to(src, dst, stage, index, target, recv_index=None):
        return pltpu.make_async_remote_copy(
            src_ref=src,
            dst_ref=dst,
            send_sem=send_sem.at[stage, index],
            recv_sem=recv_sem.at[stage, index if recv_index is None else recv_index],
            device_id=target,
            device_id_type=MESH,
        )

    def send(*args):
        copy = copy_to(*args)
        copy.start()
        started.append(copy)
        return copy

    end = HALO + length
    width = end + HALO
    pl.semaphore_wait(barrier, len(partners) + ZN - jnp.where(at_home, 1, 0))
    halo = [
        send(codes_hbm.at[:, pl.ds(0, HALO)], xb.at[:, pl.ds(end, HALO)], 0, 0, left_id),
        send(codes_hbm.at[:, pl.ds(length - HALO, HALO)], xb.at[:, pl.ds(0, HALO)], 0, 1, right_id),
    ]
    for load in loads:
        load.wait()
    pb[:, HALO:end] = dot(maps[...], rec[...])
    halo += [
        send(pb.at[:, pl.ds(HALO, HALO)], pb.at[:, pl.ds(end, HALO)], 0, 2, left_id),
        send(pb.at[:, pl.ds(end - 128, 128)], pb.at[:, pl.ds(128, 128)], 0, 3, right_id),
    ]
    pb[:, :128] = jnp.zeros((atoms, 128), F32)

    live = iota((1, slots), 1) < jnp.broadcast_to(counts_row[...], (1, slots))
    ids = jnp.where(live, ids_row[...].astype(F32), -1.0)
    tags[...] = jnp.broadcast_to(jnp.concatenate([ids] * GROUP, axis=1), tags.shape)
    select = (iota((slots, atoms), 1).astype(F32) == to_column(ids)).astype(BF)

    half = atoms // 2
    lanes = 8 * half
    pick_lag = iota((64, 8 * lanes), 1)
    pick_lag = over(pick_lag, lanes) * 8 + over(within(pick_lag, lanes), half)
    pick_lag = (pick_lag == iota((64, 8 * lanes), 0)).astype(BF)
    same = (iota((half, lanes), 0) == within(iota((half, lanes), 1), half)).astype(F32)
    spread = [dot(v, pick_lag) for v in split(waves[...])]
    filters = []
    for g in range(2):
        high, low = [
            jnp.concatenate(
                [
                    (v[g * half : (g + 1) * half, i * lanes : (i + 1) * lanes] * same).astype(BF)
                    for i in range(8)
                ],
                axis=0,
            )
            for v in spread
        ]
        filters.append(jnp.concatenate([high, high, low], axis=1))
    high, low = split(dot(maps[...], maps[...], ((1,), (1,))))
    gram = jnp.concatenate([high, high, low], axis=1)
    step = to_column(step_row[...])
    thresh = to_column(thresh_row[...])

    def depthwise(v, sign):
        n = v.shape[1]
        rolled = [
            [u if j == 0 else pltpu.roll(u, (sign * j) % n, 1) for j in range(8)] for u in split(v)
        ]
        groups = []
        for g in range(2):
            high, low = [
                jnp.concatenate([u[g * half : (g + 1) * half] for u in us], axis=0) for us in rolled
            ]
            w = dot(filters[g], jnp.concatenate([high, low, high], axis=0))
            total = w[:half]
            for i in range(1, 8):
                total = total + pltpu.roll(w[i * half : (i + 1) * half], (sign * 8 * i) % n, 1)
            groups.append(total)
        return jnp.concatenate(groups, axis=0)

    def mix(v):
        high, low = split(depthwise(v, 1))
        return dot(gram, jnp.concatenate([high, low, high], axis=0))

    inner_mix = mix(xb[:, HALO:end])
    inner_back = depthwise(pb[:, HALO:end] - inner_mix, -1)
    for copy in halo[:2]:
        copy.wait_recv()
    first = jnp.where(shard == 0, HALO, 0)
    last = jnp.where(shard == shards - 1, end, width + HALO)

    def column(start, stop):
        return iota((atoms, stop - start), 1) + start

    windows = [((128, width), (128, 1408)), ((128, 1408), (128, 1408)), ((HALO, 1408), (HALO, end))]
    v = jnp.where(column(0, width) < first, 0.0, xb[...])
    v_from = 0
    for (r_from, r_to), (c_from, c_to) in windows:
        if v_from == 0:
            outer = mix(jnp.concatenate([v[:, :384], v[:, end - 128 :]], axis=1))
            mixed = jnp.concatenate(
                [outer[:, 128:384], inner_mix[:, 128:], outer[:, 512:]], axis=1
            )
        else:
            mixed = mix(v)[:, r_from - v_from : r_to - v_from]
        if v_from == 0:
            for copy in halo[2:]:
                copy.wait_recv()
            more = [send(rec.at[:, pl.ds(0, 128)], rech, 0, 4, left_id)]
            tag_copies = [send(tags, tagr.at[o], 1, o, p) for o, (_, p) in enumerate(pairs)]
        r = pb[:, r_from:r_to] - mixed
        r = jnp.where(column(r_from, r_to) < last, r, 0.0)
        if v_from == 0:
            outer = depthwise(jnp.concatenate([r[:, :384], r[:, end - 256 :]], axis=1), -1)
            g = jnp.concatenate(
                [outer[:, :256], inner_back[:, 128 : length - 128], outer[:, 384:640]], axis=1
            )
        else:
            g = depthwise(r, -1)[:, c_from - r_from : c_to - r_from]
        v = v[:, c_from - v_from : c_to - v_from]
        v = jnp.maximum(v + step * g - thresh, 0.0)
        v = jnp.where(column(c_from, c_to) < first, 0.0, v)
        v_from = c_from

    picked = dot(select, v.astype(BF)).astype(BF)
    picked = jnp.concatenate([picked, jnp.zeros((slots, 128), BF)], axis=1)
    shifted = jnp.concatenate(
        [picked if j == 0 else pltpu.roll(picked, j, 1) for j in range(16)], axis=0
    )
    more[0].wait_recv()
    after = jnp.where(shard == shards - 1, jnp.zeros_like(rech), rech[...])
    window = jnp.concatenate([rec[...], after], axis=1)
    n = length + 128
    pieces = YN // 2
    order = [lax.rem(lax.div(y, 2) + p + 1, pieces) for p in range(pieces)]
    firsts = []
    for p in range(pieces):
        i = order[p]
        moved = pltpu.roll(window, lax.rem(n - 16 * i, n), 1)
        panel = dot(shifted, moved, ((1,), (1,)))
        panel = (panel * float(length) ** -0.5).astype(BF)
        for j in range(16):
            chunk[j % 8, 2 * i + j // 8] = panel[j * slots : (j + 1) * slots]
        rows = pl.ds(2 * i, 2)
        firsts.append(
            [
                send(chunk.at[d, rows], recv1.at[rows, me], 2 + p, o, target)
                for o, (d, target) in enumerate(pairs)
            ]
        )
        recv1[rows, me] = chunk[me, rows]

    codes_out[...] = v

    for copy in tag_copies:
        copy.wait_recv()
    lane = iota((1, GROUP * slots), 1)
    source = over(lane, slots)
    row = jnp.where(source == me, tags[:1], -1.0)
    for o in range(1, GROUP):
        frm = lax.rem(x - o // CN + XN, XN) * CN + lax.rem(core - o % CN + CN, CN)
        row = jnp.where(source == frm, tagr[o - 1, :1], row)
    expand = (iota((atoms, GROUP * slots), 0).astype(F32) == row).astype(BF)
    for p in range(pieces):
        for copy in firsts[p]:
            copy.wait_recv()
        for q in range(2):
            t = 2 * order[p] + q
            terms = recv1[t].reshape(GROUP * slots, channels)
            send2[t] = dot(expand, terms).astype(BF)
            o = lax.rem(t - y + YN, YN)

            @pl.when(o != 0)
            def _():
                copy_to(send2.at[t], recv2.at[o - 1], 6, o - 1, device(t, z, core, x)).start()

    acc = send2[y].astype(F32)
    for o in range(YN - 1):
        copy = copy_to(send2.at[0], recv2.at[o], 6, o, device(ys[0], z, core, x))
        copy.wait_recv()
        started.append(copy)
        acc = acc + recv2[o].astype(F32)
    send3[...] = acc

    third = [
        send(send3.at[pl.ds(zz * part, part)], recv3.at[o], 7, o, device(y, zz, core, x))
        for o, zz in enumerate(zs)
    ]
    acc = send3[pl.ds(pl.multiple_of(z * part, part), part)]
    for o, copy in enumerate(third):
        copy.wait_recv()
        acc = acc + recv3[o]
    tot[...] = acc

    place = x * per + lax.rem(z, per)
    fourth = []
    for o in range(ZN):
        zz = lax.rem(z + o, ZN)
        copy = copy_to(tot, recv4.at[place], 8, o, device(y, zz, core, home), place)
        fourth.append(copy)
        if o == 0:

            @pl.when(jnp.logical_not(at_home))
            def _():
                copy.start()

            @pl.when(at_home)
            def _():
                recv4[place] = tot[...]
        else:
            copy.start()
    for xx in range(XN):
        for q in range(per):
            k = xx * per + q
            copy = copy_to(tot, recv4.at[k], 8, 0, sibling, k)

            @pl.when(jnp.logical_not((x == xx) & (z == x * per + q)))
            def _():
                copy.wait_recv()

    send5[...] = recv4[...].reshape(XN * block, channels).astype(BF)
    fifth = send(send5, recv5, 9, 0, sibling)
    rows_n = YN * OWN * GROUP
    cols_n = GROUP * block
    half_n = XN * block
    block_owner = owners_row[:, :block]
    for b in range(1, XN):
        block_owner = jnp.where(x == b, owners_row[:, b * block : (b + 1) * block], block_owner)
    block_owner = jnp.concatenate([block_owner.astype(F32)] * GROUP, axis=1)
    r = iota((rows_n, cols_n), 0)
    c = iota((rows_n, cols_n), 1)
    wanted_slot = within(over(r, GROUP), OWN)
    wanted = ((over(r, OWN * GROUP) * ZN + z) * CN + core) * OWN + wanted_slot
    c_core = jnp.where(c < half_n, core, 1 - core)
    c_group = over(within(c, half_n), block) * CN + c_core
    hit = (block_owner == wanted.astype(F32)) & (within(r, GROUP) == c_group)
    hit = hit.astype(BF)
    fifth.wait_recv()

    sums = jnp.concatenate([send5[...], recv5[...]], axis=0)
    send6[...] = dot(hit, sums).astype(BF).reshape(send6.shape)
    sixth = [
        send(send6.at[yy], recv6.at[y], 10, o, device(yy, z, core, x)) for o, yy in enumerate(ys)
    ]
    recv6[y] = send6[y]
    for copy in sixth:
        copy.wait_recv()

    held = recv6[...].astype(F32)
    taps = YN * GROUP
    table = jnp.concatenate(
        [held[:, s * GROUP : (s + 1) * GROUP].reshape(taps, channels) for s in range(OWN)], axis=0
    )
    turned[...] = table.T
    even = turned[pl.ds(0, channels // 2, stride=2), :]
    odd = turned[pl.ds(1, channels // 2, stride=2), :]
    low_lanes = iota(even.shape, 1) < taps
    slot0 = jnp.where(low_lanes, even, pltpu.roll(odd, taps, 1))
    slot1 = jnp.where(low_lanes, pltpu.roll(even, taps, 1), odd)
    for q in range(channels // 2):
        panels_out[:, q * 128 : (q + 1) * 128] = jnp.concatenate(
            [slot0[q : q + 1], slot1[q : q + 1]], axis=0
        )

    for copy in started:
        copy.wait_send()
    for o, copy in enumerate(fourth):
        if o == 0:

            @pl.when(jnp.logical_not(at_home))
            def _():
                copy.wait_send()
        else:
            copy.wait_send()


def finish(codes_in, panels_in, codes_out, panels_out):
    codes_out[...] = codes_in[...]
    panels_out[...] = panels_in[...]


def body(
    recording,
    spatial_maps,
    temporal_atoms,
    codes_init,
    step_sizes,
    thresholds,
    active_ids,
    active_counts,
    owner_slots,
):
    atoms, taps = temporal_atoms.shape
    channels, length = recording.shape
    slots = active_ids.shape[1]
    width = length + 2 * HALO
    block, part = atoms // XN, atoms // ZN
    shapes = (
        jax.ShapeDtypeStruct((atoms, length), F32),
        jax.ShapeDtypeStruct((OWN, channels * taps), F32),
    )
    results = pl.pallas_call(
        kernel,
        out_shape=shapes,
        in_specs=[HBM] * 9,
        out_specs=(VMEM, VMEM),
        scratch_shapes=[
            pltpu.VMEM((channels, length), BF),
            pltpu.VMEM((atoms, channels), BF),
            pltpu.VMEM((atoms, taps), F32),
            pltpu.VMEM((1, atoms), F32),
            pltpu.VMEM((1, atoms), F32),
            pltpu.VMEM((1, slots), jnp.int32),
            pltpu.VMEM((1, 1), jnp.int32),
            pltpu.VMEM((1, atoms), jnp.int32),
            pltpu.VMEM((atoms, width), F32),
            pltpu.VMEM((atoms, width), F32),
            pltpu.VMEM((channels, 128), BF),
            pltpu.VMEM((8, GROUP * slots), F32),
            pltpu.VMEM((GROUP - 1, 8, GROUP * slots), F32),
            pltpu.VMEM((GROUP, YN, slots, channels), BF),
            pltpu.VMEM((YN, GROUP, slots, channels), BF),
            pltpu.VMEM((YN, atoms, channels), BF),
            pltpu.VMEM((YN - 1, atoms, channels), BF),
            pltpu.VMEM((atoms, channels), F32),
            pltpu.VMEM((ZN - 1, part, channels), F32),
            pltpu.VMEM((part, channels), F32),
            pltpu.VMEM((XN * block // part, part, channels), F32),
            pltpu.VMEM((XN * block, channels), BF),
            pltpu.VMEM((XN * block, channels), BF),
            pltpu.VMEM((YN, OWN * GROUP, channels), BF),
            pltpu.VMEM((YN, OWN * GROUP, channels), BF),
            pltpu.VMEM((channels, OWN * taps), F32),
            pltpu.SemaphoreType.DMA((9,)),
            pltpu.SemaphoreType.DMA((11, 8)),
            pltpu.SemaphoreType.DMA((11, 8)),
        ],
        compiler_params=pltpu.CompilerParams(
            collective_id=0, has_side_effects=True, vmem_limit_bytes=56 << 20
        ),
        name="codes_and_panels",
    )(
        recording,
        spatial_maps,
        temporal_atoms,
        codes_init,
        step_sizes.reshape(1, atoms),
        thresholds.reshape(1, atoms),
        active_ids,
        active_counts.reshape(1, 1),
        owner_slots.reshape(1, atoms),
    )
    return pl.pallas_call(
        finish,
        out_shape=shapes,
        in_specs=[VMEM] * 2,
        out_specs=(VMEM, VMEM),
        name="finish",
    )(*results)


def solution(mesh):
    in_specs = (
        P(None, ("tm", "grp")),
        P(),
        P(),
        P(None, ("tm", "grp")),
        P(),
        P(),
        P(("tm", "grp"), None),
        P(("tm", "grp")),
        P(),
    )
    out_specs = (P(None, ("tm", "grp")), P(("tm", "grp"), None))
    return jax.shard_map(body, mesh=mesh, in_specs=in_specs, out_specs=out_specs, check_vma=False)
```
